512 devices in a mesh: queue: 64 (over y, x, core), head: 8 (over z).
Axes of the slice: x: 4, y: 8, z: 8, core: 2. Of those that a mesh axis runs over, the one named last changes fastest.
Arguments:
- states: bfloat16 [16384, 3072], P('queue', 'head'), may hold values from -6 to 6
- noise: bfloat16 [512, 3072], P(None, 'head'), may hold values from -6 to 6
- w_qkv: bfloat16 [3072, 3, 3072], P('queue', None, 'head'), may hold values from -0.109375 to 0.109375
- w_out: bfloat16 [3072, 3072], P('head'), may hold values from -0.109375 to 0.109375
- w_mod: bfloat16 [256, 3, 3072], P(None, None, 'head'), may hold values from -0.375 to 0.375
- sigma_table: float32 [1000], replicated, may hold values from 0 to 1
- timesteps: int32 [64], replicated, may hold values from 0 to 999, as said below
- frame_index: int32 [64], replicated, may hold values from 0 to 127, as said below
Outputs:
- new_states: bfloat16 [16384, 3072], P('queue', 'head')
- velocity: bfloat16 [16384, 3072], P('queue', 'head')
The draws below stay inside these ranges and needn't reach their ends.
Inputs may be any that keep to these rules, and one draw needn't show every extreme that they name: `timesteps`: strictly rising along the slots; slot 0 has 0 and the last slot 999. `frame_index`: strictly rising along the slots, by 1 to 3 from slot to slot; slot 0 holds 0 and the last slot 127.
All inputs are finite; a program needn't handle non-finite values.
Results may differ from the reference program's by a relative error of at most 0.023.
Values may be sent and summed in bfloat16 or wider, within the bound.
A program may use at most 64 MiB of HBM per device.

```python
import jax
import jax.numpy as jnp
from jax import lax

D = 3072
HEADS = 24
HD = 128
TOKF = 256
TEMB = 256
TSTEPS = 1000
STEPS = 2
QUEUE = 64
HH = 3072
N_HEAD = 8


def draw_timesteps(key, part):
    key = jax.random.fold_in(key, 11)
    stride = TSTEPS // QUEUE
    extra = jax.random.randint(key, (QUEUE,), 0, stride)
    values = jnp.arange(QUEUE, dtype=jnp.int32) * stride + extra
    values = values.at[0].set(0).at[QUEUE - 1].set(TSTEPS - 1)
    return values.astype(jnp.int32)


def draw_frame_index(key, part):
    key = jax.random.fold_in(key, 23)
    extra = jax.random.randint(key, (QUEUE,), 0, 2)
    values = 2 * jnp.arange(QUEUE, dtype=jnp.int32) + extra
    values = values.at[0].set(0).at[QUEUE - 1].set(2 * QUEUE - 1)
    return values.astype(jnp.int32)


def steps_of(own_key, dims, split, smallest, top_value):
    level, own = 1.0, jax.random.fold_in(own_key, 6)
    for position, shards_of in split:
        heights = jnp.exp(jax.random.uniform(jax.random.fold_in(own, position), (shards_of,), jnp.float32, smallest / len(split), top_value / len(split)))
        level = level * jnp.repeat(heights, dims[position] // shards_of).reshape([-1 if axis == position else 1 for axis in range(len(dims))])
    return level


def gaussian(key, dims, width, most, shards=(), held_as=jnp.bfloat16):
    values = width * jax.random.normal(key, dims, jnp.float32)
    if shards:
        values = values * steps_of(key, dims, shards, -0.22, 0.18)
    return jnp.clip(values, -most, most).astype(held_as)


def setup_inputs(seed: int = 0) -> dict:
    key_of = jax.random.split(jax.random.key(seed), 9)
    states = gaussian(key_of[0], (QUEUE * TOKF, D), 1.0, 6.0, ((0, 64), (1, 8)))
    noise = gaussian(key_of[1], (STEPS * TOKF, D), 1.0, 6.0, ((1, 8),))
    w_qkv = gaussian(key_of[2], (D, 3, HH), D ** -0.5, 0.109375, ((0, 64), (2, 8)))
    w_out = gaussian(key_of[3], (HH, D), HH ** -0.5, 0.109375, ((0, 8),))
    w_mod = gaussian(key_of[4], (TEMB, 3, D), TEMB ** -0.5, 0.375, ((2, 8),))
    sigma_table = jnp.clip(jax.random.uniform(key_of[5], (TSTEPS,), jnp.float32, 0.0, 1.0), 0.0, 1.0)
    timesteps = draw_timesteps(jax.random.fold_in(key_of[8], 71), 0)
    frame_index = draw_frame_index(jax.random.fold_in(key_of[8], 71), 0)
    return dict(states=states, noise=noise, w_qkv=w_qkv, w_out=w_out, w_mod=w_mod, sigma_table=sigma_table, timesteps=timesteps, frame_index=frame_index)


def sinus(value, count, first_sin):
    half = count // 2
    freq = jnp.exp(-jnp.log(10000.0) * jnp.arange(half).astype(jnp.float32) / half)
    angle = value[:, None] * freq[None, :]
    if first_sin:
        return jnp.concatenate([jnp.sin(angle), jnp.cos(angle)], axis=1)
    return jnp.concatenate([jnp.cos(angle), jnp.sin(angle)], axis=1)

def reference(states, noise, w_qkv, w_out, w_mod, sigma_table, timesteps, frame_index):
    hidden = states.reshape(QUEUE, TOKF, D)
    extended = jnp.concatenate([frame_index, frame_index[QUEUE - 1] + jnp.arange(1, STEPS + 1).astype(jnp.int32)])
    emb = sinus(timesteps.astype(jnp.float32), TEMB, False)
    modul = jnp.einsum('qe,ecd->qcd', emb, w_mod.astype(jnp.float32), precision=lax.Precision.HIGHEST)
    shift, scale, gate = (modul[:, 0], modul[:, 1], modul[:, 2])
    sig = sigma_table[timesteps]
    target = jnp.concatenate([jnp.zeros((1,), jnp.float32), sig[:-1]])
    weights = w_qkv.reshape(D, 3 * HH)
    groups = HH // N_HEAD
    valid = (jnp.arange(2 * TOKF)[None, :] < TOKF) | (jnp.arange(QUEUE)[:, None] > 0)
    velocity = None

    def one_head(block):
        query = block[0].astype(jnp.float32)
        keys = block[1].astype(jnp.float32)
        values = block[2].astype(jnp.float32)
        prev_keys = jnp.concatenate([jnp.zeros_like(keys[:1]), keys[:-1]])
        prev_values = jnp.concatenate([jnp.zeros_like(values[:1]), values[:-1]])
        all_keys = jnp.concatenate([keys, prev_keys], axis=1)
        all_values = jnp.concatenate([values, prev_values], axis=1)
        scores = jnp.einsum('qtd,qsd->qts', query, all_keys) / jnp.sqrt(jnp.float32(HD))
        scores = jnp.where(valid[:, None, :], scores, -1e+30)
        expo = jnp.exp(scores)
        probs = (expo / lax.optimization_barrier(jnp.sum(expo, axis=2, keepdims=True))).astype(jnp.bfloat16).astype(jnp.float32)
        return jnp.einsum('qts,qsd->qtd', probs, all_values).astype(jnp.bfloat16)
    for step in range(STEPS):
        frames = extended[step:step + QUEUE].astype(jnp.float32)
        u = hidden.astype(jnp.float32) + sinus(frames, D, True)[:, None, :]
        mean = lax.optimization_barrier(jnp.mean(u, axis=2, keepdims=True))
        var = lax.optimization_barrier(jnp.mean(u * u, axis=2, keepdims=True)) - mean * mean
        normed = (u - mean) / jnp.sqrt(var + 1e-06)
        modded = (normed * (1.0 + scale[:, None, :]) + shift[:, None, :]).astype(jnp.bfloat16)
        qkv = jnp.dot(modded.reshape(QUEUE * TOKF, D), weights, preferred_element_type=jnp.float32)
        qkv = qkv.astype(jnp.bfloat16).reshape(QUEUE, TOKF, 3, HEADS, HD)
        heads_first = jnp.transpose(qkv, (3, 2, 0, 1, 4))
        attn = lax.map(one_head, heads_first)
        attn = jnp.transpose(attn, (1, 2, 0, 3)).reshape(QUEUE * TOKF, HH)
        summed = jnp.zeros((QUEUE * TOKF, D), jnp.float32)
        for member in range(N_HEAD):
            part = attn[:, member * groups:(member + 1) * groups]
            term = jnp.dot(part, w_out[member * groups:(member + 1) * groups], preferred_element_type=jnp.float32)
            term = lax.optimization_barrier(term.astype(jnp.bfloat16))
            summed = summed + term.astype(jnp.float32)
        summed = summed.reshape(QUEUE, TOKF, D)
        vel = gate[:, None, :] * summed
        velocity = vel.astype(jnp.bfloat16)
        updated = (hidden.astype(jnp.float32) + (target - sig)[:, None, None] * vel).astype(jnp.bfloat16)
        fresh = noise[step * TOKF:(step + 1) * TOKF][None]
        hidden = jnp.concatenate([updated[1:], fresh], axis=0)
    return (hidden.reshape(QUEUE * TOKF, D), velocity.reshape(QUEUE * TOKF, D))
```

```python
import functools
import math

import jax
import jax.numpy as jnp
import numpy as np
from jax import lax
from jax.experimental import pallas as pl
from jax.experimental.pallas import tpu as pltpu
from jax.sharding import PartitionSpec as P

MESH = pl.DeviceIdType.MESH
HD = 128
TEMB = 256
STEPS = 2
NX = 4
NY = 8
CORES = 2
LANES = 128
F32 = jnp.float32
BF16 = jnp.bfloat16


def frequencies(half):
    return np.exp(-np.log(10000.0) * np.arange(half) / half).astype(np.float32)


def kernel(
    queue_len,
    nz,
    sigma_ref,
    tsteps_ref,
    frames_ref,
    pfreq_ref,
    tfreq_ref,
    states_ref,
    wq_ref,
    wm_hbm,
    wo_hbm,
    noise_hbm,
    new_ref,
    vel_ref,
    xg,
    h,
    wg,
    wo,
    wm,
    acc,
    query,
    kv,
    prev,
    attn,
    rs_out,
    rs_in,
    upd,
    fresh,
    pos,
    sg,
    modg,
    mean_b,
    rstd_b,
    wo_sem,
    wm_sem,
    noise_sem,
    ag_send,
    ag_recv,
    w_send,
    w_recv,
    s_send,
    s_recv,
    st_send,
    st_recv,
    mod_send,
    mod_recv,
    kv_send,
    kv_recv,
    rs_send,
    rs_recv,
    sh_send,
    sh_recv,
):
    q = lax.axis_index("queue")
    z = lax.axis_index("head")
    core = lax.rem(q, CORES)
    x = lax.rem(q // CORES, NX)
    y = q // (CORES * NX)
    tokf, width = states_ref.shape
    half = tokf // 2
    full = width * nz
    tiles = width // LANES
    local_hh = wo.shape[1]
    heads = local_hh // HD

    def ring(base, offset, size):
        return lax.rem(base + offset + size, size)

    def queue_id(yy, xx, cc):
        return (yy * NX + xx) * CORES + cc

    def at_z(offset):
        return (q, ring(z, offset, nz))

    def at_x(offset):
        return (queue_id(y, ring(x, offset, NX), core), z)

    def at_y(offset):
        return (queue_id(ring(y, offset, NY), x, core), z)

    sibling = (queue_id(y, x, 1 - core), z)
    after = (ring(q, 1, queue_len), z)
    before = (ring(q, -1, queue_len), z)
    last_slot = q == queue_len - 1

    def remote(src, dst, send, recv, device):
        return pltpu.make_async_remote_copy(
            src_ref=src, dst_ref=dst, send_sem=send, recv_sem=recv, device_id=device, device_id_type=MESH
        )

    barrier = pltpu.get_barrier_semaphore()
    partners = [at_z(d) for d in range(1, nz)]
    partners += [at_x(1), at_x(-1), at_y(1), at_y(-1), sibling, after, before]
    for partner in partners:
        pl.semaphore_signal(barrier, inc=1, device_id=partner, device_id_type=MESH)

    wm_copy = pltpu.make_async_copy(wm_hbm, wm, wm_sem)
    wm_copy.start()
    wo_copies = [
        pltpu.make_async_copy(wo_hbm.at[:, b * width : (b + 1) * width], wo.at[b], wo_sem.at[b]) for b in range(nz)
    ]
    for copy in wo_copies:
        copy.start()
    noise_copy = pltpu.make_async_copy(noise_hbm, fresh, noise_sem)

    @pl.when(last_slot)
    def _():
        noise_copy.start()

    xg[0, z] = states_ref[...]
    for c in range(3):
        wg[y, x, core, :, c * local_hh : (c + 1) * local_hh] = wq_ref[c]

    tstep = tsteps_ref[q]
    sig_now = sigma_ref[tstep]
    sig_before = sigma_ref[tsteps_ref[jnp.maximum(q - 1, 0)]]
    sig_step = jnp.where(q > 0, sig_before, 0.0) - sig_now
    last_frame = frames_ref[queue_len - 1]

    block = lax.broadcasted_iota(jnp.int32, (nz, width), 0)
    for step in range(STEPS):
        ahead = q + step
        frame = jnp.where(
            ahead < queue_len, frames_ref[jnp.minimum(ahead, queue_len - 1)], last_frame + ahead - queue_len + 1
        )
        angle = frame.astype(F32) * pfreq_ref[...]
        pos[step] = jnp.where(block < nz // 2, jnp.sin(angle), jnp.cos(angle))

    def lanes(t):
        return slice(t * LANES, (t + 1) * LANES)

    def own_sums(step):
        row = pos[step, pl.ds(z, 1), :]
        sums = jnp.zeros((tokf, LANES), F32)
        squares = jnp.zeros((tokf, LANES), F32)
        for t in range(tiles):
            u = xg[step, z, :, lanes(t)].astype(F32) + row[:, lanes(t)]
            sums = sums + u
            squares = squares + u * u
        sums = jnp.sum(sums, axis=1, keepdims=True)
        squares = jnp.sum(squares, axis=1, keepdims=True)
        lane = lax.broadcasted_iota(jnp.int32, (tokf, LANES), 1)
        both = jnp.where(lane == 0, sums, jnp.where(lane == 1, squares, 0.0))
        sg[step, z] = both.T[0:8]

    def sums_copy(step, d):
        return remote(sg.at[step, z], sg.at[step, z], st_send.at[step, d], st_recv.at[step, d], at_z(d))

    def sums_arrival(step, d):
        k = ring(z, -d, nz)
        return remote(sg.at[step, k], sg.at[step, k], st_send.at[step, d], st_recv.at[step, d], at_z(d))

    def finish_sums(step):
        for d in range(1, nz):
            sums_arrival(step, d).wait_recv()
        total = sg[step, 0]
        for k in range(1, nz):
            total = total + sg[step, k]
        mean = total[0:1] / full
        var = total[1:2] / full - mean * mean
        rstd = lax.rsqrt(var + 1e-06)
        mean_b[...] = jnp.broadcast_to(mean, (LANES, tokf)).T
        rstd_b[...] = jnp.broadcast_to(rstd, (LANES, tokf)).T

    def ag_part(step, k, direction, r):
        if r < nz // 2 - 1:
            return xg.at[step, k]
        return xg.at[step, k, pl.ds(direction * half, half), :]

    def ag_copy(step, direction, r):
        k = ring(z, -r if direction == 0 else r, nz)
        ref = ag_part(step, k, direction, r)
        return remote(
            ref, ref, ag_send.at[step, direction, r], ag_recv.at[step, direction, r], at_z(1 if direction == 0 else -1)
        )

    def ag_arrival(step, direction, r):
        k = ring(z, -r - 1 if direction == 0 else r + 1, nz)
        ref = ag_part(step, k, direction, r)
        return remote(
            ref, ref, ag_send.at[step, direction, r], ag_recv.at[step, direction, r], at_z(1 if direction == 0 else -1)
        )

    def modulate(step, k):
        row = pos[step, pl.ds(k, 1), :]
        rows = modg[k]
        shift, scale = rows[0:1], 1.0 + rows[1:2]
        for t in range(tiles):
            u = xg[step, k, :, lanes(t)].astype(F32) + row[:, lanes(t)]
            normed = (u - mean_b[...]) * rstd_b[...]
            h[k, :, lanes(t)] = (normed * scale[:, lanes(t)] + shift[:, lanes(t)]).astype(BF16)

    def project(k):
        weights = wg[k].reshape(width, 3 * local_hh)
        acc[...] += jnp.dot(h[k], weights, preferred_element_type=F32)

    def w_copy(index, ref, device):
        return remote(ref, ref, w_send.at[index], w_recv.at[index], device)

    def s_copy(index, ref):
        return remote(ref, ref, s_send.at[index], s_recv.at[index], sibling)

    xr = [ring(x, k, NX) for k in range(NX)]
    yr = [ring(y, k, NY) for k in range(NY)]
    far = NY // 2

    c0_send = {
        0: (wg.at[y, x, 0], at_x(1)),
        1: (wg.at[y, x, 0], at_x(-1)),
        2: (wg.at[y, xr[3], 0], at_x(1)),
    }
    c0_recv = {0: wg.at[y, xr[3], 0], 1: wg.at[y, xr[1], 0], 2: wg.at[y, xr[2], 0]}
    for r in range(far):
        up, down = yr[-r % NY], yr[r]
        up_next, down_next = yr[(-r - 1) % NY], yr[r + 1]
        if r < far - 1:
            c0_send[3 + 2 * r] = (wg.at[up, :, 0], at_y(1))
            c0_send[4 + 2 * r] = (wg.at[down, :, 0], at_y(-1))
            c0_recv[3 + 2 * r] = wg.at[up_next, :, 0]
            c0_recv[4 + 2 * r] = wg.at[down_next, :, 0]
        else:
            c0_send[3 + 2 * r] = (wg.at[up, pl.ds(0, 2), 0], at_y(1))
            c0_send[4 + 2 * r] = (wg.at[down, pl.ds(2, 2), 0], at_y(-1))
            c0_recv[3 + 2 * r] = wg.at[up_next, pl.ds(0, 2), 0]
            c0_recv[4 + 2 * r] = wg.at[down_next, pl.ds(2, 2), 0]
    c1_send, c1_recv = {}, {}
    for r in range(far):
        up, down = yr[-r % NY], yr[r]
        up_next, down_next = yr[(-r - 1) % NY], yr[r + 1]
        if r < far - 1:
            c1_send[2 * r] = (wg.at[up, x, 1], at_y(1))
            c1_send[2 * r + 1] = (wg.at[down, x, 1], at_y(-1))
            c1_recv[2 * r] = wg.at[up_next, x, 1]
            c1_recv[2 * r + 1] = wg.at[down_next, x, 1]
        else:
            c1_send[2 * r] = (wg.at[up, x, 1, pl.ds(0, 32)], at_y(1))
            c1_send[2 * r + 1] = (wg.at[down, x, 1, pl.ds(32, 16)], at_y(-1))
            c1_recv[2 * r] = wg.at[up_next, x, 1, pl.ds(0, 32)]
            c1_recv[2 * r + 1] = wg.at[down_next, x, 1, pl.ds(32, 16)]
    c1_send[8] = (wg.at[:, x, 1], at_x(1))
    c1_send[9] = (wg.at[:, x, 1], at_x(-1))
    c1_recv[8] = wg.at[:, xr[3], 1]
    c1_recv[9] = wg.at[:, xr[1], 1]
    c1_send[10] = (wg.at[pl.ds(0, far), xr[3], 1], at_x(1))
    c1_send[11] = (wg.at[pl.ds(far, far), xr[1], 1], at_x(-1))
    c1_recv[10] = wg.at[pl.ds(0, far), xr[2], 1]
    c1_recv[11] = wg.at[pl.ds(far, far), xr[2], 1]
    c0_rows = [wg.at[yr[k], :, 0] for k in range(NY)]
    c1_rows = [wg.at[:, xr[k], 1] for k in range(NX)]

    def start0(*indices):
        for i in indices:
            w_copy(i, *c0_send[i]).start()

    def start1(*indices):
        for i in indices:
            w_copy(i, *c1_send[i]).start()

    def got0(*indices):
        for i in indices:
            w_copy(i, c0_recv[i], at_x(1)).wait_recv()

    def got1(*indices):
        for i in indices:
            w_copy(i, c1_recv[i], at_x(1)).wait_recv()

    def hand0(*indices):
        for i in indices:
            s_copy(i, c0_rows[i]).start()

    def hand1(*indices):
        for i in indices:
            s_copy(i, c1_rows[i]).start()

    def weights_stage(stage):
        @pl.when(core == 0)
        def _():
            if stage == 0:
                start0(0, 1)
            elif stage == 1:
                got0(0)
                start0(2)
                got0(1, 2)
                start0(3, 4)
                hand0(0)
            elif stage == 2:
                got0(3)
                start0(5)
                got0(4)
                start0(6)
                hand0(7, 1)
            elif stage == 3:
                got0(5)
                start0(7)
                got0(6)
                start0(8)
                hand0(6, 2)
            elif stage == 4:
                got0(7)
                start0(9)
                got0(8)
                start0(10)
                hand0(5, 3)
            else:
                got0(9, 10)
                hand0(4)
                for i in range(NX):
                    s_copy(i, c1_rows[i]).wait_recv()
                for i in range(11):
                    w_copy(i, *c0_send[i]).wait_send()
                for i in range(NY):
                    s_copy(i, c0_rows[i]).wait_send()

        @pl.when(core == 1)
        def _():
            if stage == 0:
                start1(0, 1)
            elif stage == 1:
                for r in range(3):
                    got1(2 * r)
                    start1(2 * r + 2)
                    got1(2 * r + 1)
                    start1(2 * r + 3)
                got1(6, 7)
                start1(8, 9)
                hand1(0)
            elif stage == 4:
                got1(8)
                start1(10)
                got1(9)
                start1(11)
                hand1(3, 1)
            elif stage == 5:
                got1(10, 11)
                hand1(2)
                for i in range(NY):
                    s_copy(i, c0_rows[i]).wait_recv()
                for i in range(12):
                    w_copy(i, *c1_send[i]).wait_send()
                for i in range(NX):
                    s_copy(i, c1_rows[i]).wait_send()

    own_sums(0)

    pl.semaphore_wait(barrier, len(partners))

    weights_stage(0)
    for direction in range(2):
        ag_copy(0, direction, 0).start()
    for d in range(1, nz):
        sums_copy(0, d).start()

    wm_copy.wait()
    angle = tstep.astype(F32) * tfreq_ref[...]
    emb = jnp.concatenate([jnp.cos(angle), jnp.sin(angle)], axis=1)
    high = emb.astype(BF16).astype(F32)
    middle = (emb - high).astype(BF16).astype(F32)
    low = (emb - high - middle).astype(BF16).astype(F32)
    index = lax.broadcasted_iota(jnp.int32, (16, TEMB), 0)
    parts = jnp.where(index == 0, high, jnp.where(index == 1, middle, jnp.where(index == 2, low, 0.0)))
    modg[z] = jnp.zeros((8, width), F32)
    for c in range(3):
        modul = jnp.dot(parts.astype(BF16), wm[c], preferred_element_type=F32)
        modg[z, c : c + 1, :] = jnp.sum(modul, axis=0, keepdims=True)

    def mod_copy(d):
        return remote(modg.at[z], modg.at[z], mod_send.at[d], mod_recv.at[d], at_z(d))

    def mod_arrival(d):
        k = ring(z, -d, nz)
        return remote(modg.at[k], modg.at[k], mod_send.at[d], mod_recv.at[d], at_z(d))

    for d in range(1, nz):
        mod_copy(d).start()

    acc[...] = jnp.zeros_like(acc)
    weights_stage(1)
    for d in range(1, nz):
        mod_arrival(d).wait_recv()

    for step in range(STEPS):
        if step > 0:
            for part in range(2):
                rows = pl.ds(part * half, half)
                sh_arrival = remote(
                    upd.at[0, part], xg.at[1, z, rows, :], sh_send.at[0, part], sh_recv.at[0, part], before
                )
                sh_arrival.wait_recv()

            @pl.when(last_slot)
            def _():
                noise_copy.wait()
                xg[1, z] = fresh[0:tokf]

            for direction in range(2):
                ag_copy(step, direction, 0).start()
            own_sums(step)
            for d in range(1, nz):
                sums_copy(step, d).start()
            acc[...] = jnp.zeros_like(acc)
        finish_sums(step)
        modulate(step, z)
        if step > 0:
            project(z)
        for r in range(nz // 2):
            for direction in range(2):
                ag_arrival(step, direction, r).wait_recv()
                if r < nz // 2 - 1:
                    ag_copy(step, direction, r + 1).start()
            blocks = [ring(z, -r - 1, nz), ring(z, r + 1, nz)] if r < nz // 2 - 1 else [ring(z, nz // 2, nz)]
            for k in blocks:
                modulate(step, k)
                if step > 0:
                    project(k)
            if step == 0:
                weights_stage(r + 2)
        if step == 0:

            def project_block(k, carry):
                project(k)
                return carry

            lax.fori_loop(0, nz, project_block, 0)

        for c in range(2):
            kv[step, c] = acc[:, (c + 1) * local_hh : (c + 2) * local_hh].astype(BF16)
            remote(kv.at[step, c], prev.at[step, c], kv_send.at[step, c], kv_recv.at[step, c], after).start()
        query[...] = acc[:, 0:local_hh].astype(BF16)

        def kv_arrival(c):
            return remote(kv.at[step, c], prev.at[step, c], kv_send.at[step, c], kv_recv.at[step, c], after)

        def scores(keys):
            s = lax.dot_general(
                query[:, keys[1]], keys[0][:, keys[1]], (((1,), (1,)), ((), ())), preferred_element_type=F32
            )
            return jnp.exp(s * (1.0 / math.sqrt(HD)))

        columns = [slice(i * HD, (i + 1) * HD) for i in range(heads)]
        own = [scores((kv.at[step, 0], columns[i])) for i in range(heads)]
        kv_arrival(0).wait_recv()
        behind = [
            jnp.where(q > 0, scores((prev.at[step, 0], columns[i])), 0.0) for i in range(heads)
        ]
        kv_arrival(1).wait_recv()
        for i in range(heads):
            total = jnp.sum(own[i], axis=1, keepdims=True) + jnp.sum(behind[i], axis=1, keepdims=True)
            p_own = (own[i] / total).astype(BF16)
            p_behind = (behind[i] / total).astype(BF16)
            out = jnp.dot(p_own, kv[step, 1, :, columns[i]], preferred_element_type=F32)
            out = out + jnp.dot(p_behind, prev[step, 1, :, columns[i]], preferred_element_type=F32)
            attn[:, columns[i]] = out.astype(BF16)

        if step == 0:
            for copy in wo_copies:
                copy.wait()

        def rs_term(direction, s):
            k = ring(z, -1 - s, nz) if direction == 0 else ring(z, 1 + s - nz, nz)
            rows = attn[direction * half : (direction + 1) * half, :]
            return jnp.dot(rows, wo[k], preferred_element_type=F32)

        def rs_copy(direction, s):
            return remote(
                rs_out.at[step, direction, s],
                rs_in.at[step, direction, s],
                rs_send.at[step, direction, s],
                rs_recv.at[step, direction, s],
                at_z(1 if direction == 0 else -1),
            )

        for direction in range(2):
            rs_out[step, direction, 0] = rs_term(direction, 0).astype(BF16)
            rs_copy(direction, 0).start()

        def hop(s, carry):
            terms = [rs_term(direction, s) for direction in range(2)]
            for direction in range(2):
                rs_copy(direction, s - 1).wait_recv()
                rs_out[step, direction, s] = (rs_in[step, direction, s - 1].astype(F32) + terms[direction]).astype(BF16)
                rs_copy(direction, s).start()
            return carry

        lax.fori_loop(1, nz - 1, hop, 0)
        terms = [rs_term(direction, nz - 1) for direction in range(2)]
        gate = modg[z][2:3]
        for direction in range(2):
            rows = slice(direction * half, (direction + 1) * half)
            rs_copy(direction, nz - 2).wait_recv()
            summed = rs_in[step, direction, nz - 2].astype(F32) + terms[direction]
            vel = gate * summed
            if step == STEPS - 1:
                vel_ref[rows, :] = vel.astype(BF16)
            upd[step, direction] = (xg[step, z, rows, :].astype(F32) + sig_step * vel).astype(BF16)
            if step < STEPS - 1:
                target = xg.at[step + 1, z, pl.ds(direction * half, half), :]
            else:
                target = new_ref.at[pl.ds(direction * half, half), :]
            remote(upd.at[step, direction], target, sh_send.at[step, direction], sh_recv.at[step, direction], before).start()

    for part in range(2):
        remote(
            upd.at[1, part], new_ref.at[pl.ds(part * half, half), :], sh_send.at[1, part], sh_recv.at[1, part], before
        ).wait_recv()

    @pl.when(last_slot)
    def _():
        new_ref[...] = fresh[tokf : 2 * tokf]

    for d in range(1, nz):
        mod_copy(d).wait_send()
    for step in range(STEPS):
        for d in range(1, nz):
            sums_copy(step, d).wait_send()
        for direction in range(2):
            for r in range(nz // 2):
                ag_copy(step, direction, r).wait_send()
            for s in range(nz - 1):
                remote(
                    rs_out.at[step, direction, s],
                    rs_in.at[step, direction, s],
                    rs_send.at[step, direction, s],
                    rs_recv.at[step, direction, s],
                    at_z(1 if direction == 0 else -1),
                ).wait_send()
            remote(
                upd.at[step, direction], upd.at[step, direction], sh_send.at[step, direction], sh_recv.at[step, direction], before
            ).wait_send()
        for c in range(2):
            remote(kv.at[step, c], prev.at[step, c], kv_send.at[step, c], kv_recv.at[step, c], after).wait_send()


def solution(mesh):
    queue_len, nz = mesh.shape["queue"], mesh.shape["head"]

    def shards(states, noise, w_qkv, w_out, w_mod, sigma_table, timesteps, frame_index):
        tokf, width = states.shape
        rows = w_qkv.shape[0]
        local_hh = w_out.shape[0]
        half = tokf // 2
        full = width * nz
        freq = frequencies(full // 2)
        pfreq = jnp.asarray(np.concatenate([freq, freq]).reshape(nz, width))
        tfreq = jnp.asarray(frequencies(TEMB // 2).reshape(1, TEMB // 2))
        vmem = pl.BlockSpec(memory_space=pltpu.VMEM)
        smem = pl.BlockSpec(memory_space=pltpu.SMEM)
        anywhere = pl.BlockSpec(memory_space=pl.ANY)
        dma = pltpu.SemaphoreType.DMA
        hops = nz // 2
        return pl.pallas_call(
            functools.partial(kernel, queue_len, nz),
            out_shape=(
                jax.ShapeDtypeStruct((tokf, width), BF16),
                jax.ShapeDtypeStruct((tokf, width), BF16),
            ),
            in_specs=[smem, smem, smem, vmem, vmem, vmem, vmem, anywhere, anywhere, anywhere],
            out_specs=(vmem, vmem),
            scratch_shapes=[
                pltpu.VMEM((STEPS, nz, tokf, width), BF16),
                pltpu.VMEM((nz, tokf, width), BF16),
                pltpu.VMEM((NY, NX, CORES, rows, 3 * local_hh), BF16),
                pltpu.VMEM((nz, local_hh, width), BF16),
                pltpu.VMEM((3, TEMB, width), BF16),
                pltpu.VMEM((tokf, 3 * local_hh), F32),
                pltpu.VMEM((tokf, local_hh), BF16),
                pltpu.VMEM((STEPS, 2, tokf, local_hh), BF16),
                pltpu.VMEM((STEPS, 2, tokf, local_hh), BF16),
                pltpu.VMEM((tokf, local_hh), BF16),
                pltpu.VMEM((STEPS, 2, nz - 1, half, width), BF16),
                pltpu.VMEM((STEPS, 2, nz - 1, half, width), BF16),
                pltpu.VMEM((STEPS, 2, half, width), BF16),
                pltpu.VMEM((STEPS * tokf, width), BF16),
                pltpu.VMEM((STEPS, nz, width), F32),
                pltpu.VMEM((STEPS, nz, 8, tokf), F32),
                pltpu.VMEM((nz, 8, width), F32),
                pltpu.VMEM((tokf, LANES), F32),
                pltpu.VMEM((tokf, LANES), F32),
                dma((nz,)),
                dma,
                dma,
                dma((STEPS, 2, hops)),
                dma((STEPS, 2, hops)),
                dma((12,)),
                dma((12,)),
                dma((NY,)),
                dma((NY,)),
                dma((STEPS, nz)),
                dma((STEPS, nz)),
                dma((nz,)),
                dma((nz,)),
                dma((STEPS, 2)),
                dma((STEPS, 2)),
                dma((STEPS, 2, nz - 1)),
                dma((STEPS, 2, nz - 1)),
                dma((STEPS, 2)),
                dma((STEPS, 2)),
            ],
            compiler_params=pltpu.CompilerParams(
                collective_id=0, has_side_effects=True, vmem_limit_bytes=48 * 1024 * 1024
            ),
        )(
            sigma_table,
            timesteps,
            frame_index,
            pfreq,
            tfreq,
            states,
            jnp.transpose(w_qkv, (1, 0, 2)),
            jnp.transpose(w_mod, (1, 0, 2)),
            w_out,
            noise,
        )

    in_specs = (
        P("queue", "head"),
        P(None, "head"),
        P("queue", None, "head"),
        P("head", None),
        P(None, None, "head"),
        P(),
        P(),
        P(),
    )
    out_specs = (P("queue", "head"), P("queue", "head"))
    return jax.shard_map(shards, mesh=mesh, in_specs=in_specs, out_specs=out_specs, check_vma=False)
```

```python
import functools
import math

import jax
import jax.numpy as jnp
import numpy as np
from jax import lax
from jax.experimental import pallas as pl
from jax.experimental.pallas import tpu as pltpu
from jax.sharding import PartitionSpec as P

MESH = pl.DeviceIdType.MESH
HD = 128
TEMB = 256
STEPS = 2
NX = 4
NY = 8
CORES = 2
AG_PARTS = 4
RS_PARTS = 4
LANES = 128
F32 = jnp.float32
BF16 = jnp.bfloat16


def frequencies(half):
    return np.exp(-np.log(10000.0) * np.arange(half) / half).astype(np.float32)


def kernel(
    queue_len,
    nz,
    sigma_hbm,
    tsteps_hbm,
    frames_hbm,
    pfreq_hbm,
    tfreq_hbm,
    states_hbm,
    wq_hbm,
    wm_hbm,
    wo_hbm,
    noise_hbm,
    new_ref,
    vel_ref,
    xg,
    h,
    wg,
    wo,
    wm,
    acc,
    query,
    kv,
    prev,
    attn,
    rs_out,
    rs_in,
    upd,
    term,
    fresh,
    pos,
    sg,
    modg,
    mean_b,
    rstd_b,
    sigma_ref,
    tsteps_ref,
    frames_ref,
    pfreq_ref,
    tfreq_ref,
    in_sem,
    wo_sem,
    wm_sem,
    noise_sem,
    ag_send,
    ag_recv,
    w_send,
    w_recv,
    s_send,
    s_recv,
    st_send,
    st_recv,
    mod_send,
    mod_recv,
    kv_send,
    kv_recv,
    rs_send,
    rs_recv,
    sh_send,
    sh_recv,
):
    q = lax.axis_index("queue")
    z = lax.axis_index("head")
    core = lax.rem(q, CORES)
    x = lax.rem(q // CORES, NX)
    y = q // (CORES * NX)
    tokf, width = states_hbm.shape
    half = tokf // 2
    full = width * nz
    tiles = width // LANES
    local_hh = wo.shape[1]
    heads = local_hh // HD

    def ring(base, offset, size):
        return lax.rem(base + offset + size, size)

    def queue_id(yy, xx, cc):
        return (yy * NX + xx) * CORES + cc

    def at_z(offset):
        return (q, ring(z, offset, nz))

    def at_x(offset):
        return (queue_id(y, ring(x, offset, NX), core), z)

    def at_y(offset):
        return (queue_id(ring(y, offset, NY), x, core), z)

    sibling = (queue_id(y, x, 1 - core), z)
    after = (ring(q, 1, queue_len), z)
    before = (ring(q, -1, queue_len), z)
    last_slot = q == queue_len - 1

    def remote(src, dst, send, recv, device):
        return pltpu.make_async_remote_copy(
            src_ref=src, dst_ref=dst, send_sem=send, recv_sem=recv, device_id=device, device_id_type=MESH
        )

    scalar_copies = [
        pltpu.make_async_copy(src, dst, in_sem.at[i])
        for i, (src, dst) in enumerate(
            [
                (tsteps_hbm, tsteps_ref),
                (frames_hbm, frames_ref),
                (sigma_hbm, sigma_ref),
                (pfreq_hbm, pfreq_ref),
                (tfreq_hbm, tfreq_ref),
            ]
        )
    ]
    states_copy = pltpu.make_async_copy(states_hbm, xg.at[0, z], in_sem.at[5])
    wq_copies = [
        pltpu.make_async_copy(
            wq_hbm.at[c], wg.at[y, x, core, :, c * local_hh : (c + 1) * local_hh], in_sem.at[6 + c]
        )
        for c in range(3)
    ]
    states_copy.start()
    for copy in wq_copies + scalar_copies:
        copy.start()

    barrier = pltpu.get_barrier_semaphore()
    partners = [at_z(d) for d in range(1, nz)]
    partners += [at_x(1), at_x(-1), at_y(1), at_y(-1), sibling, after, before]
    for partner in partners:
        pl.semaphore_signal(barrier, inc=1, device_id=partner, device_id_type=MESH)

    wm_copy = pltpu.make_async_copy(wm_hbm, wm, wm_sem)
    wm_copy.start()
    wo_copies = [
        pltpu.make_async_copy(wo_hbm.at[:, b * width : (b + 1) * width], wo.at[b], wo_sem.at[b]) for b in range(nz)
    ]
    for copy in wo_copies:
        copy.start()
    noise_copy = pltpu.make_async_copy(noise_hbm, fresh, noise_sem)

    @pl.when(last_slot)
    def _():
        noise_copy.start()

    for copy in scalar_copies:
        copy.wait()

    tstep = tsteps_ref[q]
    sig_now = sigma_ref[tstep]
    sig_before = sigma_ref[tsteps_ref[jnp.maximum(q - 1, 0)]]
    sig_step = jnp.where(q > 0, sig_before, 0.0) - sig_now
    last_frame = frames_ref[queue_len - 1]

    block = lax.broadcasted_iota(jnp.int32, (nz, width), 0)
    for step in range(STEPS):
        ahead = q + step
        frame = jnp.where(
            ahead < queue_len, frames_ref[jnp.minimum(ahead, queue_len - 1)], last_frame + ahead - queue_len + 1
        )
        angle = frame.astype(F32) * pfreq_ref[...]
        pos[step] = jnp.where(block < nz // 2, jnp.sin(angle), jnp.cos(angle))

    def lanes(t):
        return slice(t * LANES, (t + 1) * LANES)

    def own_sums(step):
        row = pos[step, pl.ds(z, 1), :]
        sums = jnp.zeros((tokf, LANES), F32)
        squares = jnp.zeros((tokf, LANES), F32)
        for t in range(tiles):
            u = xg[step, z, :, lanes(t)].astype(F32) + row[:, lanes(t)]
            sums = sums + u
            squares = squares + u * u
        sums = jnp.sum(sums, axis=1, keepdims=True)
        squares = jnp.sum(squares, axis=1, keepdims=True)
        lane = lax.broadcasted_iota(jnp.int32, (tokf, LANES), 1)
        both = jnp.where(lane == 0, sums, jnp.where(lane == 1, squares, 0.0))
        sg[step, z] = both.T[0:8]

    def sums_copy(step, d):
        return remote(sg.at[step, z], sg.at[step, z], st_send.at[step, d], st_recv.at[step, d], at_z(d))

    def sums_arrival(step, d):
        k = ring(z, -d, nz)
        return remote(sg.at[step, k], sg.at[step, k], st_send.at[step, d], st_recv.at[step, d], at_z(d))

    def finish_sums(step):
        for d in range(1, nz):
            sums_arrival(step, d).wait_recv()
        total = sg[step, 0]
        for k in range(1, nz):
            total = total + sg[step, k]
        mean = total[0:1] / full
        var = total[1:2] / full - mean * mean
        rstd = lax.rsqrt(var + 1e-06)
        mean_b[...] = jnp.broadcast_to(mean, (LANES, tokf)).T
        rstd_b[...] = jnp.broadcast_to(rstd, (LANES, tokf)).T

    last_hop = nz // 2 - 1
    part_rows = tokf // AG_PARTS

    def ag_goes(direction, r, part):
        return r < last_hop or part // (AG_PARTS // 2) == direction

    def ag_remote(step, direction, r, part, k):
        ref = xg.at[step, k, pl.ds(part * part_rows, part_rows), :]
        return remote(
            ref,
            ref,
            ag_send.at[step, direction, r, part],
            ag_recv.at[step, direction, r, part],
            at_z(1 if direction == 0 else -1),
        )

    def ag_copy(step, direction, r, part):
        return ag_remote(step, direction, r, part, ring(z, -r if direction == 0 else r, nz))

    def ag_arrival(step, direction, r, part):
        return ag_remote(step, direction, r, part, ring(z, -r - 1 if direction == 0 else r + 1, nz))

    def ag_forward(step, r, part):
        for direction in range(2):
            if ag_goes(direction, r, part):
                ag_arrival(step, direction, r, part).wait_recv()
                if r < last_hop and ag_goes(direction, r + 1, part):
                    ag_copy(step, direction, r + 1, part).start()

    def modulate(step, k):
        row = pos[step, pl.ds(k, 1), :]
        rows = modg[k]
        shift, scale = rows[0:1], 1.0 + rows[1:2]
        for t in range(tiles):
            u = xg[step, k, :, lanes(t)].astype(F32) + row[:, lanes(t)]
            normed = (u - mean_b[...]) * rstd_b[...]
            h[k, :, lanes(t)] = (normed * scale[:, lanes(t)] + shift[:, lanes(t)]).astype(BF16)

    def project(k):
        weights = wg[k].reshape(width, 3 * local_hh)
        acc[...] += jnp.dot(h[k], weights, preferred_element_type=F32)

    near_x = (0, 3, 1, 2)
    near_y = (0, 1, 7, 2, 6, 3, 5, 4)
    far = NY // 2

    def piece(c, dy, dx):
        return wg.at[ring(y, dy, NY), ring(x, dx, NX), c]

    def w_remote(index, ref, device):
        return remote(ref, ref, w_send.at[index], w_recv.at[index], device)

    def s_remote(c, dy, dx):
        index = near_y.index(dy) * NX + near_x.index(dx)
        ref = piece(c, dy, dx)
        return remote(ref, ref, s_send.at[index], s_recv.at[index], sibling)

    def both_x(dx):
        return at_x(1) if dx == 0 else at_x(-1)

    def both_y(direction):
        return at_y(1 if direction == 0 else -1)

    def c0_index(r, direction, i):
        return 3 + (r * 2 + direction) * NX + i

    def c0_goes(r, direction, i):
        return r < far - 1 or i % 2 == direction

    def c0_dy(r, direction):
        return (-r if direction == 0 else r) % NY

    def c0_y_copy(r, direction, i):
        return w_remote(c0_index(r, direction, i), piece(0, c0_dy(r, direction), near_x[i]), both_y(direction))

    def c0_y_arrival(r, direction, i):
        return w_remote(c0_index(r, direction, i), piece(0, c0_dy(r + 1, direction), near_x[i]), both_y(direction))

    def c0_row(i):
        for direction in range(2):
            c0_y_copy(0, direction, i).start()
        s_remote(0, 0, near_x[i]).start()

    def c0_x_copies():
        return [
            w_remote(0, piece(0, 0, 0), at_x(1)),
            w_remote(1, piece(0, 0, 0), at_x(-1)),
            w_remote(2, piece(0, 0, 3), at_x(1)),
        ]

    def c0_start():
        copies = c0_x_copies()
        copies[0].start()
        copies[1].start()
        c0_row(0)

    def c0_first_x():
        w_remote(0, piece(0, 0, 3), at_x(1)).wait_recv()
        c0_x_copies()[2].start()
        c0_row(1)
        w_remote(1, piece(0, 0, 1), at_x(-1)).wait_recv()
        c0_row(2)

    def c0_second_x():
        w_remote(2, piece(0, 0, 2), at_x(1)).wait_recv()
        c0_row(3)

    def c0_y(r, i):
        def event():
            for direction in range(2):
                if c0_goes(r, direction, i):
                    c0_y_arrival(r, direction, i).wait_recv()
                    if r < far - 1 and c0_goes(r + 1, direction, i):
                        c0_y_copy(r + 1, direction, i).start()
                    s_remote(0, c0_dy(r + 1, direction), near_x[i]).start()

        return event

    def c1_y_part(r, direction, dy):
        ref = piece(1, dy, 0)
        if r == far - 1:
            ref = ref.at[pl.ds(0, 32)] if direction == 0 else ref.at[pl.ds(32, 16)]
        return ref

    def c1_y_copy(r, direction):
        return w_remote(2 * r + direction, c1_y_part(r, direction, c0_dy(r, direction)), both_y(direction))

    def c1_y_arrival(r, direction):
        return w_remote(2 * r + direction, c1_y_part(r, direction, c0_dy(r + 1, direction)), both_y(direction))

    def c1_first(n, direction, dx):
        return w_remote(8 + direction * NY + n, piece(1, near_y[n], dx), at_x(1 if direction == 0 else -1))

    def c1_second(n, dx):
        return w_remote(24 + n, piece(1, near_y[n], dx), at_x(1 if n % 2 == 0 else -1))

    def c1_column(n):
        for direction in range(2):
            c1_first(n, direction, 0).start()
        s_remote(1, near_y[n], 0).start()

    def c1_start():
        for direction in range(2):
            c1_y_copy(0, direction).start()
        c1_column(0)

    def c1_y(r):
        def event():
            for direction in range(2):
                c1_y_arrival(r, direction).wait_recv()
                if r < far - 1:
                    c1_y_copy(r + 1, direction).start()
            if r < far - 1:
                c1_column(2 * r + 1)
                c1_column(2 * r + 2)
            else:
                c1_column(NY - 1)

        return event

    def c1_x(n):
        def event():
            c1_first(n, 0, 3).wait_recv()
            if n % 2 == 0:
                c1_second(n, 3).start()
            c1_first(n, 1, 1).wait_recv()
            if n % 2 == 1:
                c1_second(n, 1).start()
            s_remote(1, near_y[n], 3).start()
            s_remote(1, near_y[n], 1).start()

        return event

    def c1_xx(n):
        def event():
            c1_second(n, 2).wait_recv()
            s_remote(1, near_y[n], 2).start()

        return event

    c0_events = [[c0_first_x], [c0_y(0, 0)], [c0_second_x, c0_y(0, 1)], [c0_y(0, 2), c0_y(0, 3)]]
    c0_events += [[c0_y(r, i)] for r in range(1, far) for i in range(NX)]
    c1_events = [
        [c1_y(0)],
        [c1_x(0)],
        [c1_y(1)],
        [c1_x(1), c1_x(2)],
        [c1_xx(0)],
        [c1_y(2)],
        [c1_x(3), c1_x(4)],
        [c1_xx(1), c1_xx(2)],
        [c1_y(3)],
        [c1_x(5), c1_x(6)],
        [c1_xx(3)],
        [c1_xx(4)],
        [c1_x(7)],
        [c1_xx(5)],
        [c1_xx(6)],
        [c1_xx(7)],
    ]

    def weights_events(slot):
        @pl.when(core == 0)
        def _():
            for event in c0_events[slot]:
                event()

        @pl.when(core == 1)
        def _():
            for event in c1_events[slot]:
                event()

    def from_sibling(n):
        for c in range(CORES):

            @pl.when(core != c)
            def _():
                for dx in near_x:
                    s_remote(c, near_y[n], dx).wait_recv()

    def weights_drain():
        @pl.when(core == 0)
        def _():
            for copy in c0_x_copies():
                copy.wait_send()
            for r in range(far):
                for direction in range(2):
                    for i in range(NX):
                        if c0_goes(r, direction, i):
                            c0_y_copy(r, direction, i).wait_send()

        @pl.when(core == 1)
        def _():
            for r in range(far):
                for direction in range(2):
                    c1_y_copy(r, direction).wait_send()
            for n in range(NY):
                for direction in range(2):
                    c1_first(n, direction, 0).wait_send()
                c1_second(n, 3 if n % 2 == 0 else 1).wait_send()

        for c in range(CORES):

            @pl.when(core == c)
            def _():
                for dy in near_y:
                    for dx in near_x:
                        s_remote(c, dy, dx).wait_send()

    rs_rows = tokf // RS_PARTS

    def rows_of(part):
        return pl.ds(part * rs_rows, rs_rows)

    def rs_goes(direction, s, part):
        return s > 0 or part // (RS_PARTS // 2) == direction

    def rs_remote(step, direction, s, part):
        rows = rows_of(part)
        return remote(
            rs_out.at[step, direction, s, rows, :],
            rs_in.at[step, direction, s, rows, :],
            rs_send.at[step, direction, s, part],
            rs_recv.at[step, direction, s, part],
            at_z(1 if direction == 0 else -1),
        )

    def sh_copy(step, part):
        rows = rows_of(part)
        return remote(
            upd.at[step, rows, :],
            new_ref.at[rows, :] if step == STEPS - 1 else xg.at[step + 1, z, rows, :],
            sh_send.at[step, part],
            sh_recv.at[step, part],
            before,
        )

    sh_arrival = sh_copy

    states_copy.wait()
    own_sums(0)
    for copy in wq_copies:
        copy.wait()

    pl.semaphore_wait(barrier, len(partners))

    for d in range(1, nz):
        sums_copy(0, d).start()
    pl.when(core == 0)(c0_start)
    pl.when(core == 1)(c1_start)
    for part in range(AG_PARTS):
        for direction in range(2):
            ag_copy(0, direction, 0, part).start()

    wm_copy.wait()
    angle = tstep.astype(F32) * tfreq_ref[...]
    emb = jnp.concatenate([jnp.cos(angle), jnp.sin(angle)], axis=1)
    high = emb.astype(BF16).astype(F32)
    middle = (emb - high).astype(BF16).astype(F32)
    low = (emb - high - middle).astype(BF16).astype(F32)
    index = lax.broadcasted_iota(jnp.int32, (16, TEMB), 0)
    parts = jnp.where(index == 0, high, jnp.where(index == 1, middle, jnp.where(index == 2, low, 0.0)))
    modg[z] = jnp.zeros((8, width), F32)
    for c in range(3):
        modul = jnp.dot(parts.astype(BF16), wm[c], preferred_element_type=F32)
        modg[z, c : c + 1, :] = jnp.sum(modul, axis=0, keepdims=True)

    def mod_copy(d):
        return remote(modg.at[z], modg.at[z], mod_send.at[d], mod_recv.at[d], at_z(d))

    def mod_arrival(d):
        k = ring(z, -d, nz)
        return remote(modg.at[k], modg.at[k], mod_send.at[d], mod_recv.at[d], at_z(d))

    for d in range(1, nz):
        mod_copy(d).start()

    acc[...] = jnp.zeros_like(acc)
    for step in range(STEPS):
        if step > 0:
            @pl.when(jnp.logical_not(last_slot))
            def _():
                for part in range(RS_PARTS):
                    sh_arrival(0, part).wait_recv()

            @pl.when(last_slot)
            def _():
                noise_copy.wait()
                xg[1, z] = fresh[0:tokf]

            own_sums(step)
            for d in range(1, nz):
                sums_copy(step, d).start()
            for part in range(AG_PARTS):
                for direction in range(2):
                    ag_copy(step, direction, 0, part).start()
            acc[...] = jnp.zeros_like(acc)
        ready = [z]
        formed = False
        for r in range(nz // 2):
            for part in range(AG_PARTS):
                ag_forward(step, r, part)
                if step == 0 and r < last_hop:
                    weights_events(r * AG_PARTS + part)
                if (r, part) == ((nz // 2 - 2, 0) if step == 0 else (0, 0)):
                    formed = True
                    if step == 0:
                        for d in range(1, nz):
                            mod_arrival(d).wait_recv()
                    finish_sums(step)
                if ready and formed and (step == 0 or part % 2 == 1):
                    k = ready.pop(0)
                    modulate(step, k)
                    if step > 0:
                        project(k)
            ready += [ring(z, -r - 1, nz), ring(z, r + 1, nz)] if r < last_hop else [ring(z, nz // 2, nz)]
        for k in ready:
            modulate(step, k)
            if step > 0:
                project(k)
        if step == 0:
            for part in range(AG_PARTS):
                weights_events(last_hop * AG_PARTS + part)
                for n in ((0, 1), (2,), (3,), (4,))[part]:
                    from_sibling(n)
                    project(ring(y, near_y[n], NY))
            for n in range(5, NY):
                from_sibling(n)
                project(ring(y, near_y[n], NY))

        for c in range(2):
            kv[step, c] = acc[:, (c + 1) * local_hh : (c + 2) * local_hh].astype(BF16)
            remote(kv.at[step, c], prev.at[step, c], kv_send.at[step, c], kv_recv.at[step, c], after).start()
        query[...] = acc[:, 0:local_hh].astype(BF16)

        def kv_arrival(c):
            return remote(kv.at[step, c], prev.at[step, c], kv_send.at[step, c], kv_recv.at[step, c], after)

        def scores(keys):
            s = lax.dot_general(
                query[:, keys[1]], keys[0][:, keys[1]], (((1,), (1,)), ((), ())), preferred_element_type=F32
            )
            return jnp.exp(s * (1.0 / math.sqrt(HD)))

        columns = [slice(i * HD, (i + 1) * HD) for i in range(heads)]
        own = [scores((kv.at[step, 0], columns[i])) for i in range(heads)]
        kv_arrival(0).wait_recv()
        behind = [
            jnp.where(q > 0, scores((prev.at[step, 0], columns[i])), 0.0) for i in range(heads)
        ]
        kv_arrival(1).wait_recv()
        for i in range(heads):
            total = jnp.sum(own[i], axis=1, keepdims=True) + jnp.sum(behind[i], axis=1, keepdims=True)
            p_own = (own[i] / total).astype(BF16)
            p_behind = (behind[i] / total).astype(BF16)
            out = jnp.dot(p_own, kv[step, 1, :, columns[i]], preferred_element_type=F32)
            out = out + jnp.dot(p_behind, prev[step, 1, :, columns[i]], preferred_element_type=F32)
            attn[:, columns[i]] = out.astype(BF16)

        if step == 0:
            for copy in wo_copies:
                copy.wait()

        def rs_term(direction, s, first, count):
            k = ring(z, nz // 2 - s if direction == 0 else s - nz // 2, nz)
            return jnp.dot(attn[first : first + count, :], wo[k], preferred_element_type=F32)

        for s in range(2):
            for direction in range(2):
                side = direction if s == 0 else 1 - direction
                rs_out[step, direction, s, side * half : (side + 1) * half, :] = rs_term(
                    direction, s, side * half, half
                ).astype(BF16)
                for part in range(RS_PARTS):
                    if part // (RS_PARTS // 2) == side:
                        rs_remote(step, direction, s, part).start()
        for s in range(1, nz // 2):
            for direction in range(2):
                if s == 1:
                    rows = slice(direction * half, (direction + 1) * half)
                    term[direction, rows, :] = rs_term(direction, s, direction * half, half)
                else:
                    term[direction] = rs_term(direction, s, 0, tokf)
            for i in range(RS_PARTS):
                for direction in range(2):
                    part = (i + RS_PARTS // 2 * (1 - direction)) % RS_PARTS
                    if rs_goes(direction, s - 1, part):
                        rows = rows_of(part)
                        rs_remote(step, direction, s - 1, part).wait_recv()
                        rs_out[step, direction, s, rows, :] = (
                            rs_in[step, direction, s - 1, rows, :].astype(F32) + term[direction, rows, :]
                        ).astype(BF16)
                        rs_remote(step, direction, s, part).start()
        term[0] = rs_term(0, nz // 2, 0, tokf)
        gate = modg[z][2:3]
        for part in (2, 0, 3, 1):
            rows = rows_of(part)
            summed = term[0, rows, :]
            for direction in range(2):
                rs_remote(step, direction, nz // 2 - 1, part).wait_recv()
                summed = summed + rs_in[step, direction, nz // 2 - 1, rows, :].astype(F32)
            vel = gate * summed
            if step == STEPS - 1:
                vel_ref[rows, :] = vel.astype(BF16)
            upd[step, rows, :] = (xg[step, z, rows, :].astype(F32) + sig_step * vel).astype(BF16)

            @pl.when(q > 0)
            def _():
                sh_copy(step, part).start()

    @pl.when(last_slot)
    def _():
        new_ref[...] = fresh[tokf : 2 * tokf]

    @pl.when(jnp.logical_not(last_slot))
    def _():
        for part in range(RS_PARTS):
            sh_arrival(1, part).wait_recv()

    weights_drain()
    for d in range(1, nz):
        mod_copy(d).wait_send()
    for step in range(STEPS):
        for d in range(1, nz):
            sums_copy(step, d).wait_send()
        for direction in range(2):
            for part in range(AG_PARTS):
                for r in range(nz // 2):
                    if ag_goes(direction, r, part):
                        ag_copy(step, direction, r, part).wait_send()
            for part in range(RS_PARTS):
                for hop in range(nz // 2):
                    if rs_goes(direction, hop, part):
                        rs_remote(step, direction, hop, part).wait_send()
        for c in range(2):
            remote(kv.at[step, c], prev.at[step, c], kv_send.at[step, c], kv_recv.at[step, c], after).wait_send()

    @pl.when(q > 0)
    def _():
        for step in range(STEPS):
            for part in range(RS_PARTS):
                sh_copy(step, part).wait_send()


def solution(mesh):
    queue_len, nz = mesh.shape["queue"], mesh.shape["head"]

    def shards(states, noise, w_qkv, w_out, w_mod, sigma_table, timesteps, frame_index):
        tokf, width = states.shape
        rows = w_qkv.shape[0]
        local_hh = w_out.shape[0]
        full = width * nz
        freq = frequencies(full // 2)
        pfreq = jnp.asarray(np.concatenate([freq, freq]).reshape(nz, width))
        tfreq = jnp.asarray(frequencies(TEMB // 2).reshape(1, TEMB // 2))
        vmem = pl.BlockSpec(memory_space=pltpu.VMEM)
        anywhere = pl.BlockSpec(memory_space=pl.ANY)
        dma = pltpu.SemaphoreType.DMA
        hops = nz // 2
        return pl.pallas_call(
            functools.partial(kernel, queue_len, nz),
            out_shape=(
                jax.ShapeDtypeStruct((tokf, width), BF16),
                jax.ShapeDtypeStruct((tokf, width), BF16),
            ),
            in_specs=[anywhere] * 10,
            out_specs=(vmem, vmem),
            scratch_shapes=[
                pltpu.VMEM((STEPS, nz, tokf, width), BF16),
                pltpu.VMEM((nz, tokf, width), BF16),
                pltpu.VMEM((NY, NX, CORES, rows, 3 * local_hh), BF16),
                pltpu.VMEM((nz, local_hh, width), BF16),
                pltpu.VMEM((3, TEMB, width), BF16),
                pltpu.VMEM((tokf, 3 * local_hh), F32),
                pltpu.VMEM((tokf, local_hh), BF16),
                pltpu.VMEM((STEPS, 2, tokf, local_hh), BF16),
                pltpu.VMEM((STEPS, 2, tokf, local_hh), BF16),
                pltpu.VMEM((tokf, local_hh), BF16),
                pltpu.VMEM((STEPS, 2, hops, tokf, width), BF16),
                pltpu.VMEM((STEPS, 2, hops, tokf, width), BF16),
                pltpu.VMEM((STEPS, tokf, width), BF16),
                pltpu.VMEM((2, tokf, width), F32),
                pltpu.VMEM((STEPS * tokf, width), BF16),
                pltpu.VMEM((STEPS, nz, width), F32),
                pltpu.VMEM((STEPS, nz, 8, tokf), F32),
                pltpu.VMEM((nz, 8, width), F32),
                pltpu.VMEM((tokf, LANES), F32),
                pltpu.VMEM((tokf, LANES), F32),
                pltpu.SMEM(sigma_table.shape, F32),
                pltpu.SMEM(timesteps.shape, jnp.int32),
                pltpu.SMEM(frame_index.shape, jnp.int32),
                pltpu.VMEM(pfreq.shape, F32),
                pltpu.VMEM(tfreq.shape, F32),
                dma((9,)),
                dma((nz,)),
                dma,
                dma,
                dma((STEPS, 2, hops, AG_PARTS)),
                dma((STEPS, 2, hops, AG_PARTS)),
                dma((35,)),
                dma((35,)),
                dma((NY * NX,)),
                dma((NY * NX,)),
                dma((STEPS, nz)),
                dma((STEPS, nz)),
                dma((nz,)),
                dma((nz,)),
                dma((STEPS, 2)),
                dma((STEPS, 2)),
                dma((STEPS, 2, hops, RS_PARTS)),
                dma((STEPS, 2, hops, RS_PARTS)),
                dma((STEPS, RS_PARTS)),
                dma((STEPS, RS_PARTS)),
            ],
            compiler_params=pltpu.CompilerParams(
                collective_id=0, has_side_effects=True, vmem_limit_bytes=60 * 1024 * 1024
            ),
        )(
            sigma_table,
            timesteps,
            frame_index,
            pfreq,
            tfreq,
            states,
            jnp.transpose(w_qkv, (1, 0, 2)),
            jnp.transpose(w_mod, (1, 0, 2)),
            w_out,
            noise,
        )

    in_specs = (
        P("queue", "head"),
        P(None, "head"),
        P("queue", None, "head"),
        P("head", None),
        P(None, None, "head"),
        P(),
        P(),
        P(),
    )
    out_specs = (P("queue", "head"), P("queue", "head"))
    return jax.shard_map(shards, mesh=mesh, in_specs=in_specs, out_specs=out_specs, check_vma=False)
```

```python
import functools
import math

import jax
import jax.numpy as jnp
import numpy as np
from jax import lax
from jax.experimental import pallas as pl
from jax.experimental.pallas import tpu as pltpu
from jax.sharding import PartitionSpec as P

MESH = pl.DeviceIdType.MESH
HD = 128
TEMB = 256
STEPS = 2
NX = 4
NY = 8
CORES = 2
PARTS = 4
LATER_PARTS = (2, 0, 3, 1)
LANES = 128
F32 = jnp.float32
BF16 = jnp.bfloat16


def frequencies(half):
    return np.exp(-np.log(10000.0) * np.arange(half) / half).astype(np.float32)


def kernel(
    queue_len,
    nz,
    sigma_hbm,
    tsteps_hbm,
    frames_hbm,
    pfreq_hbm,
    tfreq_hbm,
    states_hbm,
    wq_hbm,
    wm_hbm,
    wo_hbm,
    noise_hbm,
    new_ref,
    vel_ref,
    xg,
    h,
    wkv,
    wqr,
    wo,
    wm,
    acc,
    query,
    kv,
    prev,
    attn,
    rs_out,
    rs_in,
    upd,
    term,
    fresh,
    pos,
    sg,
    modg,
    gate_ref,
    mean_b,
    rstd_b,
    sigma_ref,
    tsteps_ref,
    frames_ref,
    pfreq_ref,
    tfreq_ref,
    in_sem,
    wo_sem,
    wm_sem,
    noise_sem,
    ag_send,
    ag_recv,
    w_send,
    w_recv,
    s_send,
    s_recv,
    st_send,
    st_recv,
    mod_send,
    mod_recv,
    kv_send,
    kv_recv,
    rs_send,
    rs_recv,
    sh_send,
    sh_recv,
):
    q = lax.axis_index("queue")
    z = lax.axis_index("head")
    core = lax.rem(q, CORES)
    x = lax.rem(q // CORES, NX)
    y = q // (CORES * NX)
    tokf, width = states_hbm.shape
    half = tokf // 2
    full = width * nz
    tiles = width // LANES
    local_hh = wo.shape[1]
    heads = local_hh // HD

    def ring(base, offset, size):
        return lax.rem(base + offset + size, size)

    def queue_id(yy, xx, cc):
        return (yy * NX + xx) * CORES + cc

    def at_z(offset):
        return (q, ring(z, offset, nz))

    def at_x(offset):
        return (queue_id(y, ring(x, offset, NX), core), z)

    def at_y(offset):
        return (queue_id(ring(y, offset, NY), x, core), z)

    sibling = (queue_id(y, x, 1 - core), z)
    after = (ring(q, 1, queue_len), z)
    before = (ring(q, -1, queue_len), z)
    last_slot = q == queue_len - 1

    def remote(src, dst, send, recv, device):
        return pltpu.make_async_remote_copy(
            src_ref=src, dst_ref=dst, send_sem=send, recv_sem=recv, device_id=device, device_id_type=MESH
        )

    scalar_copies = [
        pltpu.make_async_copy(src, dst, in_sem.at[i])
        for i, (src, dst) in enumerate(
            [
                (tsteps_hbm, tsteps_ref),
                (frames_hbm, frames_ref),
                (sigma_hbm, sigma_ref),
                (pfreq_hbm, pfreq_ref),
                (tfreq_hbm, tfreq_ref),
            ]
        )
    ]
    states_copy = pltpu.make_async_copy(states_hbm, xg.at[0, z], in_sem.at[5])
    wq_copies = [
        pltpu.make_async_copy(wq_hbm.at[0], wqr.at[y, x, core], in_sem.at[6]),
        pltpu.make_async_copy(wq_hbm.at[1], wkv.at[y, x, core, :, 0:local_hh], in_sem.at[7]),
        pltpu.make_async_copy(wq_hbm.at[2], wkv.at[y, x, core, :, local_hh : 2 * local_hh], in_sem.at[8]),
    ]
    states_copy.start()
    for copy in wq_copies + scalar_copies:
        copy.start()

    barrier = pltpu.get_barrier_semaphore()
    partners = [at_z(d) for d in range(1, nz)]
    partners += [at_x(1), at_x(-1), at_x(2), at_y(1), at_y(-1), sibling, after, before]
    for partner in partners:
        pl.semaphore_signal(barrier, inc=1, device_id=partner, device_id_type=MESH)

    wm_copy = pltpu.make_async_copy(wm_hbm, wm, wm_sem)
    wm_copy.start()
    wo_copies = [
        pltpu.make_async_copy(wo_hbm.at[:, b * width : (b + 1) * width], wo.at[b], wo_sem.at[b]) for b in range(nz)
    ]
    for copy in wo_copies:
        copy.start()
    noise_copy = pltpu.make_async_copy(noise_hbm, fresh, noise_sem)

    @pl.when(last_slot)
    def _():
        noise_copy.start()

    for copy in scalar_copies:
        copy.wait()

    tstep = tsteps_ref[q]
    sig_now = sigma_ref[tstep]
    sig_before = sigma_ref[tsteps_ref[jnp.maximum(q - 1, 0)]]
    sig_step = jnp.where(q > 0, sig_before, 0.0) - sig_now
    last_frame = frames_ref[queue_len - 1]

    block = lax.broadcasted_iota(jnp.int32, (nz, width), 0)
    for step in range(STEPS):
        ahead = q + step
        frame = jnp.where(
            ahead < queue_len, frames_ref[jnp.minimum(ahead, queue_len - 1)], last_frame + ahead - queue_len + 1
        )
        angle = frame.astype(F32) * pfreq_ref[...]
        pos[step] = jnp.where(block < nz // 2, jnp.sin(angle), jnp.cos(angle))

    def lanes(t):
        return slice(t * LANES, (t + 1) * LANES)

    def own_sums(step):
        row = pos[step, pl.ds(z, 1), :]
        sums = jnp.zeros((tokf, LANES), F32)
        squares = jnp.zeros((tokf, LANES), F32)
        for t in range(tiles):
            u = xg[step, z, :, lanes(t)].astype(F32) + row[:, lanes(t)]
            sums = sums + u
            squares = squares + u * u
        sums = jnp.sum(sums, axis=1, keepdims=True)
        squares = jnp.sum(squares, axis=1, keepdims=True)
        lane = lax.broadcasted_iota(jnp.int32, (tokf, LANES), 1)
        both = jnp.where(lane == 0, sums, jnp.where(lane == 1, squares, 0.0))
        sg[step, z] = both.T[0:2]

    def sums_copy(step, d):
        return remote(sg.at[step, z], sg.at[step, z], st_send.at[step, d], st_recv.at[step, d], at_z(d))

    def sums_arrival(step, d):
        k = ring(z, -d, nz)
        return remote(sg.at[step, k], sg.at[step, k], st_send.at[step, d], st_recv.at[step, d], at_z(d))

    def finish_sums(step):
        for d in range(1, nz):
            sums_arrival(step, d).wait_recv()
        total = sg[step, 0]
        for k in range(1, nz):
            total = total + sg[step, k]
        mean = total[0:1] / full
        var = total[1:2] / full - mean * mean
        rstd = lax.rsqrt(var + 1e-06)
        mean_b[...] = jnp.broadcast_to(mean, (LANES, tokf)).T
        rstd_b[...] = jnp.broadcast_to(rstd, (LANES, tokf)).T

    last_hop = nz // 2 - 1
    part_rows = tokf // PARTS

    def ag_goes(direction, r, part):
        return r < last_hop or part // (PARTS // 2) == direction

    def ag_remote(step, direction, r, part, k):
        ref = xg.at[step, k, pl.ds(part * part_rows, part_rows), :]
        return remote(
            ref,
            ref,
            ag_send.at[step, direction, r, part],
            ag_recv.at[step, direction, r, part],
            at_z(1 if direction == 0 else -1),
        )

    def ag_copy(step, direction, r, part):
        return ag_remote(step, direction, r, part, ring(z, -r if direction == 0 else r, nz))

    def ag_arrival(step, direction, r, part):
        return ag_remote(step, direction, r, part, ring(z, -r - 1 if direction == 0 else r + 1, nz))

    def ag_forward(step, r, part):
        for direction in range(2):
            if ag_goes(direction, r, part):
                ag_arrival(step, direction, r, part).wait_recv()
                if r < last_hop and ag_goes(direction, r + 1, part):
                    ag_copy(step, direction, r + 1, part).start()

    def modulate(step, k):
        row = pos[step, pl.ds(k, 1), :]
        rows = modg[k]
        shift, scale = rows[0:1], 1.0 + rows[1:2]
        for t in range(tiles):
            u = xg[step, k, :, lanes(t)].astype(F32) + row[:, lanes(t)]
            normed = (u - mean_b[...]) * rstd_b[...]
            h[:, pl.ds(pl.multiple_of(k * width + t * LANES, LANES), LANES)] = (normed * scale[:, lanes(t)] + shift[:, lanes(t)]).astype(BF16)

    def block_of_h(k):
        return h[:, pl.ds(pl.multiple_of(k * width, LANES), width)]

    def project_kv(k):
        weights = wkv[k].reshape(width, 2 * local_hh)
        acc[:, local_hh:] += jnp.dot(block_of_h(k), weights, preferred_element_type=F32)

    def project_query(k):
        weights = wqr[k].reshape(width, local_hh)
        acc[:, :local_hh] += jnp.dot(block_of_h(k), weights, preferred_element_type=F32)

    near_x = (0, 3, 1, 2)
    near_y = (0, 1, 7, 2, 6, 3, 5, 4)
    far = NY // 2

    def piece(g, c, dy, dx):
        return (wqr if g else wkv).at[ring(y, dy, NY), ring(x, dx, NX), c]

    def w_remote(g, index, ref, device):
        return remote(ref, ref, w_send.at[g, index], w_recv.at[g, index], device)

    def s_remote(g, c, dy, dx):
        index = near_y.index(dy) * NX + near_x.index(dx)
        ref = piece(g, c, dy, dx)
        return remote(ref, ref, s_send.at[g, index], s_recv.at[g, index], sibling)

    def both_x(dx):
        return at_x(1) if dx == 0 else at_x(-1)

    def both_y(direction):
        return at_y(1 if direction == 0 else -1)

    def c0_index(r, direction, i):
        return 3 + (r * 2 + direction) * NX + i

    def c0_goes(r, direction, i):
        return r < far - 1 or i % 2 == direction

    def c0_dy(r, direction):
        return (-r if direction == 0 else r) % NY

    def half_piece(ref, direction):
        return ref.at[pl.ds(0, 32)] if direction == 0 else ref.at[pl.ds(32, 16)]

    def c0_y_copy(g, r, direction, i):
        return w_remote(g, c0_index(r, direction, i), piece(g, 0, c0_dy(r, direction), near_x[i]), both_y(direction))

    def c0_y_arrival(g, r, direction, i):
        return w_remote(g, c0_index(r, direction, i), piece(g, 0, c0_dy(r + 1, direction), near_x[i]), both_y(direction))

    def c0_row(g, i):
        for direction in range(2):
            c0_y_copy(g, 0, direction, i).start()
        s_remote(g, 0, 0, near_x[i]).start()

    def c0_x_copies(g):
        return [
            w_remote(g, 0, piece(g, 0, 0, 0), at_x(1)),
            w_remote(g, 1, piece(g, 0, 0, 0), at_x(-1)),
            w_remote(g, 2, piece(g, 0, 0, 0), at_x(2)),
        ]

    def c0_start(g):
        for copy in c0_x_copies(g):
            copy.start()
        c0_row(g, 0)

    def c0_first_x(g):
        w_remote(g, 0, piece(g, 0, 0, 3), at_x(1)).wait_recv()
        c0_row(g, 1)
        w_remote(g, 1, piece(g, 0, 0, 1), at_x(-1)).wait_recv()
        c0_row(g, 2)

    def c0_second_x(g):
        w_remote(g, 2, piece(g, 0, 0, 2), at_x(1)).wait_recv()
        c0_row(g, 3)

    def c0_y(g, r, i):
        def event():
            for direction in range(2):
                if c0_goes(r, direction, i):
                    c0_y_arrival(g, r, direction, i).wait_recv()
                    if r < far - 1 and c0_goes(r + 1, direction, i):
                        c0_y_copy(g, r + 1, direction, i).start()
                    s_remote(g, 0, c0_dy(r + 1, direction), near_x[i]).start()

        return event

    def c1_y_part(g, r, direction, dy):
        ref = piece(g, 1, dy, 0)
        return half_piece(ref, direction) if r == far - 1 else ref

    def c1_y_copy(g, r, direction):
        return w_remote(g, 2 * r + direction, c1_y_part(g, r, direction, c0_dy(r, direction)), both_y(direction))

    def c1_y_arrival(g, r, direction):
        return w_remote(g, 2 * r + direction, c1_y_part(g, r, direction, c0_dy(r + 1, direction)), both_y(direction))

    def c1_first(g, n, direction, dx):
        return w_remote(g, 8 + direction * NY + n, piece(g, 1, near_y[n], dx), at_x(1 if direction == 0 else -1))

    def c1_second(g, n, dx):
        return w_remote(g, 24 + n, piece(g, 1, near_y[n], dx), at_x(1 if n % 2 == 0 else -1))

    def c1_column(g, n):
        for direction in range(2):
            c1_first(g, n, direction, 0).start()
        s_remote(g, 1, near_y[n], 0).start()

    def c1_start(g):
        for direction in range(2):
            c1_y_copy(g, 0, direction).start()
        c1_column(g, 0)

    def c1_y(g, r):
        def event():
            for direction in range(2):
                c1_y_arrival(g, r, direction).wait_recv()
                if r < far - 1:
                    c1_y_copy(g, r + 1, direction).start()

        return event

    def c1_send(g, n):
        def event():
            c1_column(g, n)

        return event

    def c1_x(g, n):
        def event():
            c1_first(g, n, 0, 3).wait_recv()
            if n % 2 == 0:
                c1_second(g, n, 3).start()
            c1_first(g, n, 1, 1).wait_recv()
            if n % 2 == 1:
                c1_second(g, n, 1).start()
            s_remote(g, 1, near_y[n], 3).start()
            s_remote(g, 1, near_y[n], 1).start()

        return event

    def c1_xx(g, n):
        def event():
            c1_second(g, n, 2).wait_recv()
            s_remote(g, 1, near_y[n], 2).start()

        return event

    def c0_events(g):
        return [
            [functools.partial(c0_first_x, g)],
            [c0_y(g, 0, 0)],
            [functools.partial(c0_second_x, g)],
            [c0_y(g, 0, 1)],
            [c0_y(g, 0, 2)],
            [c0_y(g, 1, 0)],
            [c0_y(g, 0, 3)],
            [c0_y(g, 1, 1)],
            [c0_y(g, 1, 2)],
            [c0_y(g, 2, 0)],
            [c0_y(g, 1, 3)],
            [c0_y(g, 2, 1)],
            [c0_y(g, 2, 2)],
            [c0_y(g, 3, 0)],
            [c0_y(g, 2, 3)],
            [c0_y(g, 3, 1)],
            [c0_y(g, 3, 2)],
            [c0_y(g, 3, 3)],
        ]

    def c1_events(g):
        return [
            [c1_y(g, 0)],
            [c1_x(g, 0), c1_send(g, 1)],
            [],
            [c1_y(g, 1), c1_send(g, 2)],
            [c1_x(g, 1), c1_send(g, 3)],
            [c1_xx(g, 0), c1_x(g, 2), c1_send(g, 4)],
            [],
            [c1_y(g, 2)],
            [c1_x(g, 3), c1_send(g, 5)],
            [c1_xx(g, 1), c1_x(g, 4), c1_send(g, 6)],
            [c1_xx(g, 2)],
            [c1_y(g, 3)],
            [c1_x(g, 5), c1_send(g, 7)],
            [c1_xx(g, 3), c1_x(g, 6)],
            [c1_xx(g, 4)],
            [c1_x(g, 7)],
            [c1_xx(g, 5), c1_xx(g, 6)],
            [c1_xx(g, 7)],
        ]

    def weights_events(g, slot):
        @pl.when(core == 0)
        def _():
            for event in c0_events(g)[slot]:
                event()

        @pl.when(core == 1)
        def _():
            for event in c1_events(g)[slot]:
                event()

    def from_sibling(g, n):
        for c in range(CORES):

            @pl.when(core != c)
            def _():
                for dx in near_x:
                    s_remote(g, c, near_y[n], dx).wait_recv()

    def weights_drain(g):
        @pl.when(core == 0)
        def _():
            for copy in c0_x_copies(g):
                copy.wait_send()
            for r in range(far):
                for direction in range(2):
                    for i in range(NX):
                        if c0_goes(r, direction, i):
                            c0_y_copy(g, r, direction, i).wait_send()

        @pl.when(core == 1)
        def _():
            for r in range(far):
                for direction in range(2):
                    c1_y_copy(g, r, direction).wait_send()
            for n in range(NY):
                for direction in range(2):
                    c1_first(g, n, direction, 0).wait_send()
                c1_second(g, n, 3 if n % 2 == 0 else 1).wait_send()

        for c in range(CORES):

            @pl.when(core == c)
            def _():
                for dy in near_y:
                    for dx in near_x:
                        s_remote(g, c, dy, dx).wait_send()

    first_order = [
        "w0", "w1", "w2", "v0", "a00", "v1", "v2", "a01", "w3", "a02", "w4", "a03", "w5", "w6", "a10", "v3",
        "v4", "a11", "w7", "v5", "v6", "a12", "w8", "a13", "w9", "v7", "w10", "v8", "a20", "a21", "w11", "v9",
        "a22", "w12", "v10", "a23", "w13", "v11", "m", "w14", "v12", "a30", "w15", "v13", "a31", "w16", "v14", "a32",
        "w17", "v15", "a33", "v16", "m", "k", "s", "v17", "q",
    ]
    later_order = ["a%d%d" % (r, part) for r in range(nz // 2) for part in LATER_PARTS]

    rs_rows = tokf // PARTS

    def rows_of(part):
        return pl.ds(part * rs_rows, rs_rows)

    def rs_goes(direction, s, part):
        return s > 0 or part // (PARTS // 2) == direction

    def rs_remote(step, direction, s, part):
        rows = rows_of(part)
        return remote(
            rs_out.at[step, direction, s, rows, :],
            rs_in.at[step, direction, s, rows, :],
            rs_send.at[step, direction, s, part],
            rs_recv.at[step, direction, s, part],
            at_z(1 if direction == 0 else -1),
        )

    def sh_copy(step, part):
        rows = rows_of(part)
        return remote(
            upd.at[step, rows, :],
            new_ref.at[rows, :] if step == STEPS - 1 else xg.at[step + 1, z, rows, :],
            sh_send.at[step, part],
            sh_recv.at[step, part],
            before,
        )

    sh_arrival = sh_copy

    states_copy.wait()
    own_sums(0)
    for copy in wq_copies:
        copy.wait()

    pl.semaphore_wait(barrier, len(partners))

    for d in range(1, nz):
        sums_copy(0, d).start()
    for g in range(2):
        pl.when(core == 0)(functools.partial(c0_start, g))
        pl.when(core == 1)(functools.partial(c1_start, g))
    for part in range(PARTS):
        for direction in range(2):
            ag_copy(0, direction, 0, part).start()

    wm_copy.wait()
    angle = tstep.astype(F32) * tfreq_ref[...]
    emb = jnp.concatenate([jnp.cos(angle), jnp.sin(angle)], axis=1)
    high = emb.astype(BF16).astype(F32)
    middle = (emb - high).astype(BF16).astype(F32)
    low = (emb - high - middle).astype(BF16).astype(F32)
    index = lax.broadcasted_iota(jnp.int32, (16, TEMB), 0)
    parts = jnp.where(index == 0, high, jnp.where(index == 1, middle, jnp.where(index == 2, low, 0.0)))
    for c in range(3):
        modul = jnp.dot(parts.astype(BF16), wm[c], preferred_element_type=F32)
        modul = jnp.sum(modul, axis=0, keepdims=True)
        if c < 2:
            modg[z, c : c + 1, :] = modul
        else:
            gate_ref[...] = modul

    def mod_copy(d):
        return remote(modg.at[z], modg.at[z], mod_send.at[d], mod_recv.at[d], at_z(d))

    def mod_arrival(d):
        k = ring(z, -d, nz)
        return remote(modg.at[k], modg.at[k], mod_send.at[d], mod_recv.at[d], at_z(d))

    for d in range(1, nz):
        mod_copy(d).start()

    acc[...] = jnp.zeros_like(acc)
    def begin(step):
        @pl.when(last_slot)
        def _():
            noise_copy.wait()
            xg[step, z] = fresh[(step - 1) * tokf : step * tokf]

        for part in LATER_PARTS:

            @pl.when(jnp.logical_not(last_slot))
            def _():
                sh_arrival(step - 1, part).wait_recv()

            for direction in range(2):
                ag_copy(step, direction, 0, part).start()
        own_sums(step)
        for d in range(1, nz):
            sums_copy(step, d).start()

    for step in range(STEPS):
        if step > 0:
            acc[...] = jnp.zeros_like(acc)
        def kv_arrival(c):
            return remote(kv.at[step, c], prev.at[step, c], kv_send.at[step, c], kv_recv.at[step, c], after)

        def send_kv():
            for c in range(2):
                kv[step, c] = acc[:, (c + 1) * local_hh : (c + 2) * local_hh].astype(BF16)
                kv_arrival(c).start()

        ready = [z]
        formed = False
        for i, item in enumerate(first_order if step == 0 else later_order):
            kind, number = item[0], int(item[1:] or 0)
            if kind in "wv":
                weights_events("wv".index(kind), number)
            elif kind in "kq":
                for n in range(NY):
                    from_sibling("kq".index(kind), n)
                if kind == "k":
                    acc[:, local_hh:] = jnp.dot(
                        h[...], wkv[...].reshape(full, 2 * local_hh), preferred_element_type=F32
                    )
                else:
                    acc[:, :local_hh] = jnp.dot(
                        h[...], wqr[...].reshape(full, local_hh), preferred_element_type=F32
                    )
            elif kind == "m":
                if not formed:
                    formed = True
                    for d in range(1, nz):
                        mod_arrival(d).wait_recv()
                    finish_sums(step)
                for k in ready:
                    modulate(step, k)
                ready = []
            elif kind == "s":
                send_kv()
            else:
                r, part = number // 10, number % 10
                ag_forward(step, r, part)
                if step > 0 and i == PARTS + 1:
                    formed = True
                    finish_sums(step)
                if step > 0 and ready and formed:
                    k = ready.pop(0)
                    modulate(step, k)
                    project_kv(k)
                    project_query(k)
                if part == (PARTS - 1 if step == 0 else LATER_PARTS[-1]):
                    ready += [ring(z, -r - 1, nz), ring(z, r + 1, nz)] if r < last_hop else [ring(z, nz // 2, nz)]
        if step > 0:
            for k in ready:
                modulate(step, k)
                project_kv(k)
            send_kv()
            for k in ready:
                project_query(k)
        query[...] = acc[:, 0:local_hh].astype(BF16)

        def scores(keys):
            s = lax.dot_general(
                query[:, keys[1]], keys[0][:, keys[1]], (((1,), (1,)), ((), ())), preferred_element_type=F32
            )
            return jnp.exp(s * (1.0 / math.sqrt(HD)))

        columns = [slice(i * HD, (i + 1) * HD) for i in range(heads)]
        own = [scores((kv.at[step, 0], columns[i])) for i in range(heads)]
        kv_arrival(0).wait_recv()
        behind = [
            jnp.where(q > 0, scores((prev.at[step, 0], columns[i])), 0.0) for i in range(heads)
        ]
        kv_arrival(1).wait_recv()
        for i in range(heads):
            total = jnp.sum(own[i], axis=1, keepdims=True) + jnp.sum(behind[i], axis=1, keepdims=True)
            p_own = (own[i] / total).astype(BF16)
            p_behind = (behind[i] / total).astype(BF16)
            out = jnp.dot(p_own, kv[step, 1, :, columns[i]], preferred_element_type=F32)
            out = out + jnp.dot(p_behind, prev[step, 1, :, columns[i]], preferred_element_type=F32)
            attn[:, columns[i]] = out.astype(BF16)

        if step == 0:
            for copy in wo_copies:
                copy.wait()

        def rs_term(direction, s, first, count):
            k = ring(z, nz // 2 - s if direction == 0 else s - nz // 2, nz)
            return jnp.dot(attn[first : first + count, :], wo[k], preferred_element_type=F32)

        for s in range(2):
            for direction in range(2):
                side = direction if s == 0 else 1 - direction
                rs_out[step, direction, s, side * half : (side + 1) * half, :] = rs_term(
                    direction, s, side * half, half
                ).astype(BF16)
                for part in range(PARTS):
                    if part // (PARTS // 2) == side:
                        rs_remote(step, direction, s, part).start()
        for s in range(1, nz // 2):
            for direction in range(2):
                if s == 1:
                    rows = slice(direction * half, (direction + 1) * half)
                    term[s, direction, rows, :] = rs_term(direction, s, direction * half, half)
                else:
                    term[s, direction] = rs_term(direction, s, 0, tokf)
        term[0, 0] = rs_term(0, nz // 2, 0, tokf)
        for s in range(1, nz // 2):
            for i in range(PARTS):
                for direction in range(2):
                    part = (i + PARTS // 2 * (1 - direction)) % PARTS
                    if rs_goes(direction, s - 1, part):
                        rows = rows_of(part)
                        rs_remote(step, direction, s - 1, part).wait_recv()
                        rs_out[step, direction, s, rows, :] = (
                            rs_in[step, direction, s - 1, rows, :].astype(F32) + term[s, direction, rows, :]
                        ).astype(BF16)
                        rs_remote(step, direction, s, part).start()
        if step < STEPS - 1:
            pl.when(core == 0)(functools.partial(begin, step + 1))
        gate = gate_ref[...]
        for part in LATER_PARTS:
            rows = rows_of(part)
            summed = term[0, 0, rows, :]
            for direction in range(2):
                rs_remote(step, direction, nz // 2 - 1, part).wait_recv()
                summed = summed + rs_in[step, direction, nz // 2 - 1, rows, :].astype(F32)
            vel = gate * summed
            if step == STEPS - 1:
                vel_ref[rows, :] = vel.astype(BF16)
            upd[step, rows, :] = (xg[step, z, rows, :].astype(F32) + sig_step * vel).astype(BF16)

            @pl.when(q > 0)
            def _():
                sh_copy(step, part).start()

        if step < STEPS - 1:
            pl.when(core == 1)(functools.partial(begin, step + 1))

    @pl.when(last_slot)
    def _():
        new_ref[...] = fresh[tokf : 2 * tokf]

    @pl.when(jnp.logical_not(last_slot))
    def _():
        for part in range(PARTS):
            sh_arrival(1, part).wait_recv()

    for g in range(2):
        weights_drain(g)
    for d in range(1, nz):
        mod_copy(d).wait_send()
    for step in range(STEPS):
        for d in range(1, nz):
            sums_copy(step, d).wait_send()
        for direction in range(2):
            for part in range(PARTS):
                for r in range(nz // 2):
                    if ag_goes(direction, r, part):
                        ag_copy(step, direction, r, part).wait_send()
            for part in range(PARTS):
                for hop in range(nz // 2):
                    if rs_goes(direction, hop, part):
                        rs_remote(step, direction, hop, part).wait_send()
        for c in range(2):
            remote(kv.at[step, c], prev.at[step, c], kv_send.at[step, c], kv_recv.at[step, c], after).wait_send()

    @pl.when(q > 0)
    def _():
        for step in range(STEPS):
            for part in range(PARTS):
                sh_copy(step, part).wait_send()


def solution(mesh):
    queue_len, nz = mesh.shape["queue"], mesh.shape["head"]

    def shards(states, noise, w_qkv, w_out, w_mod, sigma_table, timesteps, frame_index):
        tokf, width = states.shape
        rows = w_qkv.shape[0]
        local_hh = w_out.shape[0]
        full = width * nz
        freq = frequencies(full // 2)
        pfreq = jnp.asarray(np.concatenate([freq, freq]).reshape(nz, width))
        tfreq = jnp.asarray(frequencies(TEMB // 2).reshape(1, TEMB // 2))
        vmem = pl.BlockSpec(memory_space=pltpu.VMEM)
        anywhere = pl.BlockSpec(memory_space=pl.ANY)
        dma = pltpu.SemaphoreType.DMA
        hops = nz // 2
        return pl.pallas_call(
            functools.partial(kernel, queue_len, nz),
            out_shape=(
                jax.ShapeDtypeStruct((tokf, width), BF16),
                jax.ShapeDtypeStruct((tokf, width), BF16),
            ),
            in_specs=[anywhere] * 10,
            out_specs=(vmem, vmem),
            scratch_shapes=[
                pltpu.VMEM((STEPS, nz, tokf, width), BF16),
                pltpu.VMEM((tokf, nz * width), BF16),
                pltpu.VMEM((NY, NX, CORES, rows, 2 * local_hh), BF16),
                pltpu.VMEM((NY, NX, CORES, rows, local_hh), BF16),
                pltpu.VMEM((nz, local_hh, width), BF16),
                pltpu.VMEM((3, TEMB, width), BF16),
                pltpu.VMEM((tokf, 3 * local_hh), F32),
                pltpu.VMEM((tokf, local_hh), BF16),
                pltpu.VMEM((STEPS, 2, tokf, local_hh), BF16),
                pltpu.VMEM((STEPS, 2, tokf, local_hh), BF16),
                pltpu.VMEM((tokf, local_hh), BF16),
                pltpu.VMEM((STEPS, 2, hops, tokf, width), BF16),
                pltpu.VMEM((STEPS, 2, hops, tokf, width), BF16),
                pltpu.VMEM((STEPS, tokf, width), BF16),
                pltpu.VMEM((hops, 2, tokf, width), F32),
                pltpu.VMEM((STEPS * tokf, width), BF16),
                pltpu.VMEM((STEPS, nz, width), F32),
                pltpu.VMEM((STEPS, nz, 2, tokf), F32),
                pltpu.VMEM((nz, 2, width), F32),
                pltpu.VMEM((1, width), F32),
                pltpu.VMEM((tokf, LANES), F32),
                pltpu.VMEM((tokf, LANES), F32),
                pltpu.SMEM(sigma_table.shape, F32),
                pltpu.SMEM(timesteps.shape, jnp.int32),
                pltpu.SMEM(frame_index.shape, jnp.int32),
                pltpu.VMEM(pfreq.shape, F32),
                pltpu.VMEM(tfreq.shape, F32),
                dma((9,)),
                dma((nz,)),
                dma,
                dma,
                dma((STEPS, 2, hops, PARTS)),
                dma((STEPS, 2, hops, PARTS)),
                dma((2, 35)),
                dma((2, 35)),
                dma((2, NY * NX)),
                dma((2, NY * NX)),
                dma((STEPS, nz)),
                dma((STEPS, nz)),
                dma((nz,)),
                dma((nz,)),
                dma((STEPS, 2)),
                dma((STEPS, 2)),
                dma((STEPS, 2, hops, PARTS)),
                dma((STEPS, 2, hops, PARTS)),
                dma((STEPS, PARTS)),
                dma((STEPS, PARTS)),
            ],
            compiler_params=pltpu.CompilerParams(
                collective_id=0, has_side_effects=True, vmem_limit_bytes=60 * 1024 * 1024
            ),
        )(
            sigma_table,
            timesteps,
            frame_index,
            pfreq,
            tfreq,
            states,
            jnp.transpose(w_qkv, (1, 0, 2)),
            jnp.transpose(w_mod, (1, 0, 2)),
            w_out,
            noise,
        )

    in_specs = (
        P("queue", "head"),
        P(None, "head"),
        P("queue", None, "head"),
        P("head", None),
        P(None, None, "head"),
        P(),
        P(),
        P(),
    )
    out_specs = (P("queue", "head"), P("queue", "head"))
    return jax.shard_map(shards, mesh=mesh, in_specs=in_specs, out_specs=out_specs, check_vma=False)
```

```python
import functools
import math

import jax
import jax.numpy as jnp
import numpy as np
from jax import lax
from jax.experimental import pallas as pl
from jax.experimental.pallas import tpu as pltpu
from jax.sharding import PartitionSpec as P

MESH = pl.DeviceIdType.MESH
HD = 128
TEMB = 256
STEPS = 2
NX = 4
NY = 8
CORES = 2
PARTS = 8
LATER_PARTS = tuple(i // 2 + (PARTS // 2 if i % 2 == 0 else 0) for i in range(PARTS))
LANES = 128
F32 = jnp.float32
BF16 = jnp.bfloat16


def frequencies(half):
    return np.exp(-np.log(10000.0) * np.arange(half) / half).astype(np.float32)


def kernel(
    queue_len,
    nz,
    sigma_hbm,
    tsteps_hbm,
    frames_hbm,
    pfreq_hbm,
    tfreq_hbm,
    states_hbm,
    wq_hbm,
    wm_hbm,
    wo_hbm,
    noise_hbm,
    new_ref,
    vel_ref,
    xg,
    h,
    wkv,
    wqr,
    wo,
    wm,
    acc,
    query,
    kv,
    prev,
    attn,
    rs_out,
    rs_in,
    upd,
    term,
    fresh,
    pos,
    sg,
    modg,
    gate_ref,
    mean_b,
    rstd_b,
    sigma_ref,
    tsteps_ref,
    frames_ref,
    pfreq_ref,
    tfreq_ref,
    in_sem,
    wo_sem,
    wm_sem,
    noise_sem,
    ag_send,
    ag_recv,
    w_send,
    w_recv,
    s_send,
    s_recv,
    st_send,
    st_recv,
    mod_send,
    mod_recv,
    kv_send,
    kv_recv,
    rs_send,
    rs_recv,
    sh_send,
    sh_recv,
):
    q = lax.axis_index("queue")
    z = lax.axis_index("head")
    core = lax.rem(q, CORES)
    x = lax.rem(q // CORES, NX)
    y = q // (CORES * NX)
    tokf, width = states_hbm.shape
    half = tokf // 2
    full = width * nz
    tiles = width // LANES
    local_hh = wo.shape[1]
    heads = local_hh // HD

    def ring(base, offset, size):
        return lax.rem(base + offset + size, size)

    def queue_id(yy, xx, cc):
        return (yy * NX + xx) * CORES + cc

    def at_z(offset):
        return (q, ring(z, offset, nz))

    def at_x(offset):
        return (queue_id(y, ring(x, offset, NX), core), z)

    def at_y(offset):
        return (queue_id(ring(y, offset, NY), x, core), z)

    sibling = (queue_id(y, x, 1 - core), z)
    after = (ring(q, 1, queue_len), z)
    before = (ring(q, -1, queue_len), z)
    last_slot = q == queue_len - 1

    def remote(src, dst, send, recv, device):
        return pltpu.make_async_remote_copy(
            src_ref=src, dst_ref=dst, send_sem=send, recv_sem=recv, device_id=device, device_id_type=MESH
        )

    scalar_copies = [
        pltpu.make_async_copy(src, dst, in_sem.at[i])
        for i, (src, dst) in enumerate(
            [
                (tsteps_hbm, tsteps_ref),
                (frames_hbm, frames_ref),
                (sigma_hbm, sigma_ref),
                (pfreq_hbm, pfreq_ref),
                (tfreq_hbm, tfreq_ref),
            ]
        )
    ]
    states_copy = pltpu.make_async_copy(states_hbm, xg.at[0, z], in_sem.at[5])
    wq_copies = [
        pltpu.make_async_copy(wq_hbm.at[0], wqr.at[y, x, core], in_sem.at[6]),
        pltpu.make_async_copy(wq_hbm.at[1], wkv.at[y, x, core, :, 0:local_hh], in_sem.at[7]),
        pltpu.make_async_copy(wq_hbm.at[2], wkv.at[y, x, core, :, local_hh : 2 * local_hh], in_sem.at[8]),
    ]
    states_copy.start()
    for copy in wq_copies + scalar_copies:
        copy.start()

    barrier = pltpu.get_barrier_semaphore()
    partners = [at_z(d) for d in range(1, nz)]
    partners += [at_x(1), at_x(-1), at_x(2), at_y(1), at_y(-1), sibling, after, before]
    for partner in partners:
        pl.semaphore_signal(barrier, inc=1, device_id=partner, device_id_type=MESH)

    wm_copy = pltpu.make_async_copy(wm_hbm, wm, wm_sem)
    wm_copy.start()
    wo_copies = [
        pltpu.make_async_copy(wo_hbm.at[:, b * width : (b + 1) * width], wo.at[b], wo_sem.at[b]) for b in range(nz)
    ]
    for copy in wo_copies:
        copy.start()
    noise_copy = pltpu.make_async_copy(noise_hbm, fresh, noise_sem)

    @pl.when(last_slot)
    def _():
        noise_copy.start()

    for copy in scalar_copies:
        copy.wait()

    tstep = tsteps_ref[q]
    sig_now = sigma_ref[tstep]
    sig_before = sigma_ref[tsteps_ref[jnp.maximum(q - 1, 0)]]
    sig_step = jnp.where(q > 0, sig_before, 0.0) - sig_now
    last_frame = frames_ref[queue_len - 1]

    block = lax.broadcasted_iota(jnp.int32, (nz, width), 0)
    for step in range(STEPS):
        ahead = q + step
        frame = jnp.where(
            ahead < queue_len, frames_ref[jnp.minimum(ahead, queue_len - 1)], last_frame + ahead - queue_len + 1
        )
        angle = frame.astype(F32) * pfreq_ref[...]
        pos[step] = jnp.where(block < nz // 2, jnp.sin(angle), jnp.cos(angle))

    def lanes(t):
        return slice(t * LANES, (t + 1) * LANES)

    def own_sums(step):
        row = pos[step, pl.ds(z, 1), :]
        sums = jnp.zeros((tokf, LANES), F32)
        squares = jnp.zeros((tokf, LANES), F32)
        for t in range(tiles):
            u = xg[step, z, :, lanes(t)].astype(F32) + row[:, lanes(t)]
            sums = sums + u
            squares = squares + u * u
        sums = jnp.sum(sums, axis=1, keepdims=True)
        squares = jnp.sum(squares, axis=1, keepdims=True)
        lane = lax.broadcasted_iota(jnp.int32, (tokf, LANES), 1)
        both = jnp.where(lane == 0, sums, jnp.where(lane == 1, squares, 0.0))
        sg[step, z] = both.T[0:2]

    def sums_copy(step, d):
        return remote(sg.at[step, z], sg.at[step, z], st_send.at[step, d], st_recv.at[step, d], at_z(d))

    def sums_arrival(step, d):
        k = ring(z, -d, nz)
        return remote(sg.at[step, k], sg.at[step, k], st_send.at[step, d], st_recv.at[step, d], at_z(d))

    def finish_sums(step):
        for d in range(1, nz):
            sums_arrival(step, d).wait_recv()
        total = sg[step, 0]
        for k in range(1, nz):
            total = total + sg[step, k]
        mean = total[0:1] / full
        var = total[1:2] / full - mean * mean
        rstd = lax.rsqrt(var + 1e-06)
        mean_b[...] = jnp.broadcast_to(mean, (LANES, tokf)).T
        rstd_b[...] = jnp.broadcast_to(rstd, (LANES, tokf)).T

    last_hop = nz // 2 - 1
    part_rows = tokf // PARTS

    def ag_goes(direction, r, part):
        return r < last_hop or part // (PARTS // 2) == direction

    def ag_remote(step, direction, r, part, k):
        ref = xg.at[step, k, pl.ds(part * part_rows, part_rows), :]
        return remote(
            ref,
            ref,
            ag_send.at[step, direction, r, part],
            ag_recv.at[step, direction, r, part],
            at_z(1 if direction == 0 else -1),
        )

    def ag_copy(step, direction, r, part):
        return ag_remote(step, direction, r, part, ring(z, -r if direction == 0 else r, nz))

    def ag_arrival(step, direction, r, part):
        return ag_remote(step, direction, r, part, ring(z, -r - 1 if direction == 0 else r + 1, nz))

    def ag_forward(step, r, part):
        for direction in range(2):
            if ag_goes(direction, r, part):
                ag_arrival(step, direction, r, part).wait_recv()
                if r < last_hop and ag_goes(direction, r + 1, part):
                    ag_copy(step, direction, r + 1, part).start()

    def modulate(step, k):
        row = pos[step, pl.ds(k, 1), :]
        rows = modg[k]
        shift, scale = rows[0:1], 1.0 + rows[1:2]
        for t in range(tiles):
            u = xg[step, k, :, lanes(t)].astype(F32) + row[:, lanes(t)]
            normed = (u - mean_b[...]) * rstd_b[...]
            h[:, pl.ds(pl.multiple_of(k * width + t * LANES, LANES), LANES)] = (normed * scale[:, lanes(t)] + shift[:, lanes(t)]).astype(BF16)

    def block_of_h(k):
        return h[:, pl.ds(pl.multiple_of(k * width, LANES), width)]

    def project_kv(k):
        weights = wkv[k].reshape(width, 2 * local_hh)
        acc[:, local_hh:] += jnp.dot(block_of_h(k), weights, preferred_element_type=F32)

    def project_last(k, c):
        weights = wkv[k, :, :, :, c * local_hh : (c + 1) * local_hh].reshape(width, local_hh)
        total = acc[:, (c + 1) * local_hh : (c + 2) * local_hh]
        return (total + jnp.dot(block_of_h(k), weights, preferred_element_type=F32)).astype(BF16)

    def project_query(k):
        weights = wqr[k].reshape(width, local_hh)
        acc[:, :local_hh] += jnp.dot(block_of_h(k), weights, preferred_element_type=F32)

    near_x = (0, 3, 1, 2)
    near_y = (0, 1, 7, 2, 6, 3, 5, 4)
    far = NY // 2

    def piece(g, c, dy, dx):
        return (wqr if g else wkv).at[ring(y, dy, NY), ring(x, dx, NX), c]

    def w_remote(g, index, ref, device):
        return remote(ref, ref, w_send.at[g, index], w_recv.at[g, index], device)

    def s_remote(g, c, dy, dx):
        index = near_y.index(dy) * NX + near_x.index(dx)
        ref = piece(g, c, dy, dx)
        return remote(ref, ref, s_send.at[g, index], s_recv.at[g, index], sibling)

    def both_x(dx):
        return at_x(1) if dx == 0 else at_x(-1)

    def both_y(direction):
        return at_y(1 if direction == 0 else -1)

    def c0_index(r, direction, i):
        return 3 + (r * 2 + direction) * NX + i

    def c0_goes(r, direction, i):
        return r < far - 1 or i % 2 == direction

    def c0_dy(r, direction):
        return (-r if direction == 0 else r) % NY

    def half_piece(ref, direction):
        return ref.at[pl.ds(0, 32)] if direction == 0 else ref.at[pl.ds(32, 16)]

    def c0_y_copy(g, r, direction, i):
        return w_remote(g, c0_index(r, direction, i), piece(g, 0, c0_dy(r, direction), near_x[i]), both_y(direction))

    def c0_y_arrival(g, r, direction, i):
        return w_remote(g, c0_index(r, direction, i), piece(g, 0, c0_dy(r + 1, direction), near_x[i]), both_y(direction))

    def c0_row(g, i):
        for direction in range(2):
            c0_y_copy(g, 0, direction, i).start()
        s_remote(g, 0, 0, near_x[i]).start()

    def c0_x_copies(g):
        return [
            w_remote(g, 0, piece(g, 0, 0, 0), at_x(1)),
            w_remote(g, 1, piece(g, 0, 0, 0), at_x(-1)),
            w_remote(g, 2, piece(g, 0, 0, 0), at_x(2)),
        ]

    def c0_start(g):
        for copy in c0_x_copies(g):
            copy.start()
        c0_row(g, 0)

    def c0_first_x(g):
        w_remote(g, 0, piece(g, 0, 0, 3), at_x(1)).wait_recv()
        c0_row(g, 1)
        w_remote(g, 1, piece(g, 0, 0, 1), at_x(-1)).wait_recv()
        c0_row(g, 2)

    def c0_second_x(g):
        w_remote(g, 2, piece(g, 0, 0, 2), at_x(1)).wait_recv()
        c0_row(g, 3)

    def c0_y(g, r, i):
        def event():
            for direction in range(2):
                if c0_goes(r, direction, i):
                    c0_y_arrival(g, r, direction, i).wait_recv()
                    if r < far - 1 and c0_goes(r + 1, direction, i):
                        c0_y_copy(g, r + 1, direction, i).start()
                    s_remote(g, 0, c0_dy(r + 1, direction), near_x[i]).start()

        return event

    def c1_y_part(g, r, direction, dy):
        ref = piece(g, 1, dy, 0)
        return half_piece(ref, direction) if r == far - 1 else ref

    def c1_y_copy(g, r, direction):
        return w_remote(g, 2 * r + direction, c1_y_part(g, r, direction, c0_dy(r, direction)), both_y(direction))

    def c1_y_arrival(g, r, direction):
        return w_remote(g, 2 * r + direction, c1_y_part(g, r, direction, c0_dy(r + 1, direction)), both_y(direction))

    def c1_first(g, n, direction, dx):
        return w_remote(g, 8 + direction * NY + n, piece(g, 1, near_y[n], dx), at_x(1 if direction == 0 else -1))

    def c1_second(g, n, dx):
        return w_remote(g, 24 + n, piece(g, 1, near_y[n], dx), at_x(1 if n % 2 == 0 else -1))

    def c1_column(g, n):
        for direction in range(2):
            c1_first(g, n, direction, 0).start()
        s_remote(g, 1, near_y[n], 0).start()

    def c1_start(g):
        for direction in range(2):
            c1_y_copy(g, 0, direction).start()
        c1_column(g, 0)

    def c1_y(g, r):
        def event():
            for direction in range(2):
                c1_y_arrival(g, r, direction).wait_recv()
                if r < far - 1:
                    c1_y_copy(g, r + 1, direction).start()

        return event

    def c1_send(g, n):
        def event():
            c1_column(g, n)

        return event

    def c1_x(g, n):
        def event():
            c1_first(g, n, 0, 3).wait_recv()
            if n % 2 == 0:
                c1_second(g, n, 3).start()
            c1_first(g, n, 1, 1).wait_recv()
            if n % 2 == 1:
                c1_second(g, n, 1).start()
            s_remote(g, 1, near_y[n], 3).start()
            s_remote(g, 1, near_y[n], 1).start()

        return event

    def c1_xx(g, n):
        def event():
            c1_second(g, n, 2).wait_recv()
            s_remote(g, 1, near_y[n], 2).start()

        return event

    def c0_events(g):
        return [
            [functools.partial(c0_first_x, g)],
            [c0_y(g, 0, 0)],
            [functools.partial(c0_second_x, g)],
            [c0_y(g, 0, 1)],
            [c0_y(g, 0, 2)],
            [c0_y(g, 1, 0)],
            [c0_y(g, 0, 3)],
            [c0_y(g, 1, 1)],
            [c0_y(g, 1, 2)],
            [c0_y(g, 2, 0)],
            [c0_y(g, 1, 3)],
            [c0_y(g, 2, 1)],
            [c0_y(g, 2, 2)],
            [c0_y(g, 3, 0)],
            [c0_y(g, 2, 3)],
            [c0_y(g, 3, 1)],
            [c0_y(g, 3, 2)],
            [c0_y(g, 3, 3)],
        ]

    def c1_events(g):
        return [
            [c1_y(g, 0)],
            [c1_x(g, 0), c1_send(g, 1)],
            [],
            [c1_y(g, 1), c1_send(g, 2)],
            [c1_x(g, 1), c1_send(g, 3)],
            [c1_xx(g, 0), c1_x(g, 2), c1_send(g, 4)],
            [],
            [c1_y(g, 2)],
            [c1_x(g, 3), c1_send(g, 5)],
            [c1_xx(g, 1), c1_x(g, 4), c1_send(g, 6)],
            [c1_xx(g, 2)],
            [c1_y(g, 3)],
            [c1_x(g, 5), c1_send(g, 7)],
            [c1_xx(g, 3), c1_x(g, 6)],
            [c1_xx(g, 4)],
            [c1_x(g, 7)],
            [c1_xx(g, 5), c1_xx(g, 6)],
            [c1_xx(g, 7)],
        ]

    def weights_events(g, slot):
        @pl.when(core == 0)
        def _():
            for event in c0_events(g)[slot]:
                event()

        @pl.when(core == 1)
        def _():
            for event in c1_events(g)[slot]:
                event()

    def from_sibling(g, n):
        for c in range(CORES):

            @pl.when(core != c)
            def _():
                for dx in near_x:
                    s_remote(g, c, near_y[n], dx).wait_recv()

    def weights_drain(g):
        @pl.when(core == 0)
        def _():
            for copy in c0_x_copies(g):
                copy.wait_send()
            for r in range(far):
                for direction in range(2):
                    for i in range(NX):
                        if c0_goes(r, direction, i):
                            c0_y_copy(g, r, direction, i).wait_send()

        @pl.when(core == 1)
        def _():
            for r in range(far):
                for direction in range(2):
                    c1_y_copy(g, r, direction).wait_send()
            for n in range(NY):
                for direction in range(2):
                    c1_first(g, n, direction, 0).wait_send()
                c1_second(g, n, 3 if n % 2 == 0 else 1).wait_send()

        for c in range(CORES):

            @pl.when(core == c)
            def _():
                for dy in near_y:
                    for dx in near_x:
                        s_remote(g, c, dy, dx).wait_send()

    first_order = [
        "w0", "w1", "w2", "v0", "a00", "v1", "v2", "a01", "w3", "a02", "w4", "a03", "w5", "w6", "a10", "v3",
        "v4", "a11", "w7", "v5", "v6", "a12", "w8", "a13", "m", "w9", "v7", "w10", "v8", "a20", "m", "a21",
        "w11", "v9", "a22", "w12", "v10", "a23", "w13", "v11", "w14", "v12", "a30", "m", "a31", "w15", "v13", "a32",
        "a33", "m", "k0", "k1", "w16", "v14", "k2", "k3", "k4", "w17", "v15", "k5", "k6", "s", "v16", "v17",
        "q",
    ]
    later_order = ["a%d%d" % (r, part) for r in range(nz // 2) for part in LATER_PARTS]

    rs_rows = tokf // PARTS

    def rows_of(part):
        return pl.ds(part * rs_rows, rs_rows)

    def rs_goes(direction, s, part):
        return s > 0 or part // (PARTS // 2) == direction

    def rs_remote(step, direction, s, part):
        rows = rows_of(part)
        return remote(
            rs_out.at[step, direction, s, rows, :],
            rs_in.at[step, direction, s, rows, :],
            rs_send.at[step, direction, s, part],
            rs_recv.at[step, direction, s, part],
            at_z(1 if direction == 0 else -1),
        )

    def sh_copy(step, part):
        rows = rows_of(part)
        return remote(
            upd.at[step, rows, :],
            new_ref.at[rows, :] if step == STEPS - 1 else xg.at[step + 1, z, rows, :],
            sh_send.at[step, part],
            sh_recv.at[step, part],
            before,
        )

    sh_arrival = sh_copy

    states_copy.wait()
    own_sums(0)
    for copy in wq_copies:
        copy.wait()

    pl.semaphore_wait(barrier, len(partners))

    for d in range(1, nz):
        sums_copy(0, d).start()
    for g in range(2):
        pl.when(core == 0)(functools.partial(c0_start, g))
        pl.when(core == 1)(functools.partial(c1_start, g))
    for part in range(PARTS):
        for direction in range(2):
            ag_copy(0, direction, 0, part).start()

    wm_copy.wait()
    angle = tstep.astype(F32) * tfreq_ref[...]
    emb = jnp.concatenate([jnp.cos(angle), jnp.sin(angle)], axis=1)
    high = emb.astype(BF16).astype(F32)
    middle = (emb - high).astype(BF16).astype(F32)
    low = (emb - high - middle).astype(BF16).astype(F32)
    index = lax.broadcasted_iota(jnp.int32, (16, TEMB), 0)
    parts = jnp.where(index == 0, high, jnp.where(index == 1, middle, jnp.where(index == 2, low, 0.0)))
    for c in range(3):
        modul = jnp.dot(parts.astype(BF16), wm[c], preferred_element_type=F32)
        modul = jnp.sum(modul, axis=0, keepdims=True)
        if c < 2:
            modg[z, c : c + 1, :] = modul
        else:
            gate_ref[...] = modul

    def mod_copy(d):
        return remote(modg.at[z], modg.at[z], mod_send.at[d], mod_recv.at[d], at_z(d))

    def mod_arrival(d):
        k = ring(z, -d, nz)
        return remote(modg.at[k], modg.at[k], mod_send.at[d], mod_recv.at[d], at_z(d))

    for d in range(1, nz):
        mod_copy(d).start()

    acc[...] = jnp.zeros_like(acc)

    def begin(step):
        @pl.when(last_slot)
        def _():
            noise_copy.wait()
            xg[step, z] = fresh[(step - 1) * tokf : step * tokf]

        for part in LATER_PARTS:

            @pl.when(jnp.logical_not(last_slot))
            def _():
                sh_arrival(step - 1, part).wait_recv()

            for direction in range(2):
                ag_copy(step, direction, 0, part).start()
        own_sums(step)
        for d in range(1, nz):
            sums_copy(step, d).start()

    for step in range(STEPS):
        if step > 0:
            acc[...] = jnp.zeros_like(acc)

        def kv_arrival(c):
            return remote(kv.at[step, c], prev.at[step, c], kv_send.at[step, c], kv_recv.at[step, c], after)

        def send_kv(k):
            for c in range(2):
                kv[step, c] = project_last(k, c)
                kv_arrival(c).start()

        ready = [z]
        formed = False
        for i, item in enumerate(first_order if step == 0 else later_order):
            kind, number = item[0], int(item[1:] or 0)
            if kind in "wv":
                weights_events("wv".index(kind), number)
            elif kind == "k":
                from_sibling(0, number)
                project_kv(ring(y, near_y[number], NY))
            elif kind == "q":
                for n in range(NY):
                    from_sibling(1, n)
                acc[:, :local_hh] = jnp.dot(h[...], wqr[...].reshape(full, local_hh), preferred_element_type=F32)
            elif kind == "m":
                if not formed:
                    formed = True
                    for d in range(1, nz):
                        mod_arrival(d).wait_recv()
                    finish_sums(step)
                for k in ready:
                    modulate(step, k)
                ready = []
            elif kind == "s":
                from_sibling(0, NY - 1)
                send_kv(ring(y, near_y[-1], NY))
            else:
                r, part = number // 10, number % 10
                for p in range(part * PARTS // 4, (part + 1) * PARTS // 4) if step == 0 else (part,):
                    ag_forward(step, r, p)
                if step > 0 and i == PARTS + 1:
                    formed = True
                    finish_sums(step)
                if step > 0 and ready and formed:
                    k = ready.pop(0)
                    modulate(step, k)
                    project_kv(k)
                    project_query(k)
                if part == (3 if step == 0 else LATER_PARTS[-1]):
                    ready += [ring(z, -r - 1, nz), ring(z, r + 1, nz)] if r < last_hop else [ring(z, nz // 2, nz)]
        if step > 0:
            for k in ready:
                modulate(step, k)
            for k in ready[:-1]:
                project_kv(k)
            send_kv(ready[-1])
            for k in ready:
                project_query(k)
        query[...] = acc[:, 0:local_hh].astype(BF16)

        def scores(keys):
            s = lax.dot_general(
                query[:, keys[1]], keys[0][:, keys[1]], (((1,), (1,)), ((), ())), preferred_element_type=F32
            )
            return jnp.exp(s * (1.0 / math.sqrt(HD)))

        columns = [slice(i * HD, (i + 1) * HD) for i in range(heads)]
        own = [scores((kv.at[step, 0], columns[i])) for i in range(heads)]
        kv_arrival(0).wait_recv()
        behind = [
            jnp.where(q > 0, scores((prev.at[step, 0], columns[i])), 0.0) for i in range(heads)
        ]
        kv_arrival(1).wait_recv()
        for i in range(heads):
            total = jnp.sum(own[i], axis=1, keepdims=True) + jnp.sum(behind[i], axis=1, keepdims=True)
            p_own = (own[i] / total).astype(BF16)
            p_behind = (behind[i] / total).astype(BF16)
            out = jnp.dot(p_own, kv[step, 1, :, columns[i]], preferred_element_type=F32)
            out = out + jnp.dot(p_behind, prev[step, 1, :, columns[i]], preferred_element_type=F32)
            attn[:, columns[i]] = out.astype(BF16)

        if step == 0:
            for copy in wo_copies:
                copy.wait()

        def rs_term(direction, s, first, count):
            k = ring(z, nz // 2 - s if direction == 0 else s - nz // 2, nz)
            return jnp.dot(attn[first : first + count, :], wo[k], preferred_element_type=F32)

        for s in range(2):
            for direction in range(2):
                side = direction if s == 0 else 1 - direction
                rs_out[step, direction, s, side * half : (side + 1) * half, :] = rs_term(
                    direction, s, side * half, half
                ).astype(BF16)
                for part in range(PARTS):
                    if part // (PARTS // 2) == side:
                        rs_remote(step, direction, s, part).start()
        for s in range(1, nz // 2):
            for direction in range(2):
                if s == 1:
                    rows = slice(direction * half, (direction + 1) * half)
                    term[s, direction, rows, :] = rs_term(direction, s, direction * half, half)
                else:
                    term[s, direction] = rs_term(direction, s, 0, tokf)
        term[0, 0] = rs_term(0, nz // 2, 0, tokf)
        for s in range(1, nz // 2):
            for i in range(PARTS):
                for direction in range(2):
                    part = (i + PARTS // 2 * (1 - direction)) % PARTS
                    if rs_goes(direction, s - 1, part):
                        rows = rows_of(part)
                        rs_remote(step, direction, s - 1, part).wait_recv()
                        rs_out[step, direction, s, rows, :] = (
                            rs_in[step, direction, s - 1, rows, :].astype(F32) + term[s, direction, rows, :]
                        ).astype(BF16)
                        rs_remote(step, direction, s, part).start()
        if step < STEPS - 1:
            pl.when(core == 0)(functools.partial(begin, step + 1))
        gate = gate_ref[...]
        for part in LATER_PARTS:
            rows = rows_of(part)
            summed = term[0, 0, rows, :]
            for direction in range(2):
                rs_remote(step, direction, nz // 2 - 1, part).wait_recv()
                summed = summed + rs_in[step, direction, nz // 2 - 1, rows, :].astype(F32)
            vel = gate * summed
            if step == STEPS - 1:
                vel_ref[rows, :] = vel.astype(BF16)
            upd[step, rows, :] = (xg[step, z, rows, :].astype(F32) + sig_step * vel).astype(BF16)

            @pl.when(q > 0)
            def _():
                sh_copy(step, part).start()

        if step < STEPS - 1:
            pl.when(core == 1)(functools.partial(begin, step + 1))

    for g in range(2):
        weights_drain(g)
    for d in range(1, nz):
        mod_copy(d).wait_send()
    for step in range(STEPS):
        for d in range(1, nz):
            sums_copy(step, d).wait_send()
        for direction in range(2):
            for part in range(PARTS):
                for r in range(nz // 2):
                    if ag_goes(direction, r, part):
                        ag_copy(step, direction, r, part).wait_send()
            for part in range(PARTS):
                for hop in range(nz // 2):
                    if rs_goes(direction, hop, part):
                        rs_remote(step, direction, hop, part).wait_send()
        for c in range(2):
            remote(kv.at[step, c], prev.at[step, c], kv_send.at[step, c], kv_recv.at[step, c], after).wait_send()

    @pl.when(last_slot)
    def _():
        new_ref[...] = fresh[tokf : 2 * tokf]

    @pl.when(jnp.logical_not(last_slot))
    def _():
        for part in range(PARTS):
            sh_arrival(1, part).wait_recv()

    @pl.when(q > 0)
    def _():
        for step in range(STEPS):
            for part in range(PARTS):
                sh_copy(step, part).wait_send()


def solution(mesh):
    queue_len, nz = mesh.shape["queue"], mesh.shape["head"]

    def shards(states, noise, w_qkv, w_out, w_mod, sigma_table, timesteps, frame_index):
        tokf, width = states.shape
        rows = w_qkv.shape[0]
        local_hh = w_out.shape[0]
        full = width * nz
        freq = frequencies(full // 2)
        pfreq = jnp.asarray(np.concatenate([freq, freq]).reshape(nz, width))
        tfreq = jnp.asarray(frequencies(TEMB // 2).reshape(1, TEMB // 2))
        vmem = pl.BlockSpec(memory_space=pltpu.VMEM)
        anywhere = pl.BlockSpec(memory_space=pl.ANY)
        dma = pltpu.SemaphoreType.DMA
        hops = nz // 2
        return pl.pallas_call(
            functools.partial(kernel, queue_len, nz),
            out_shape=(
                jax.ShapeDtypeStruct((tokf, width), BF16),
                jax.ShapeDtypeStruct((tokf, width), BF16),
            ),
            in_specs=[anywhere] * 10,
            out_specs=(vmem, vmem),
            scratch_shapes=[
                pltpu.VMEM((STEPS, nz, tokf, width), BF16),
                pltpu.VMEM((tokf, nz * width), BF16),
                pltpu.VMEM((NY, NX, CORES, rows, 2 * local_hh), BF16),
                pltpu.VMEM((NY, NX, CORES, rows, local_hh), BF16),
                pltpu.VMEM((nz, local_hh, width), BF16),
                pltpu.VMEM((3, TEMB, width), BF16),
                pltpu.VMEM((tokf, 3 * local_hh), F32),
                pltpu.VMEM((tokf, local_hh), BF16),
                pltpu.VMEM((STEPS, 2, tokf, local_hh), BF16),
                pltpu.VMEM((STEPS, 2, tokf, local_hh), BF16),
                pltpu.VMEM((tokf, local_hh), BF16),
                pltpu.VMEM((STEPS, 2, hops, tokf, width), BF16),
                pltpu.VMEM((STEPS, 2, hops, tokf, width), BF16),
                pltpu.VMEM((STEPS, tokf, width), BF16),
                pltpu.VMEM((hops, 2, tokf, width), F32),
                pltpu.VMEM((STEPS * tokf, width), BF16),
                pltpu.VMEM((STEPS, nz, width), F32),
                pltpu.VMEM((STEPS, nz, 2, tokf), F32),
                pltpu.VMEM((nz, 2, width), F32),
                pltpu.VMEM((1, width), F32),
                pltpu.VMEM((tokf, LANES), F32),
                pltpu.VMEM((tokf, LANES), F32),
                pltpu.SMEM(sigma_table.shape, F32),
                pltpu.SMEM(timesteps.shape, jnp.int32),
                pltpu.SMEM(frame_index.shape, jnp.int32),
                pltpu.VMEM(pfreq.shape, F32),
                pltpu.VMEM(tfreq.shape, F32),
                dma((9,)),
                dma((nz,)),
                dma,
                dma,
                dma((STEPS, 2, hops, PARTS)),
                dma((STEPS, 2, hops, PARTS)),
                dma((2, 35)),
                dma((2, 35)),
                dma((2, NY * NX)),
                dma((2, NY * NX)),
                dma((STEPS, nz)),
                dma((STEPS, nz)),
                dma((nz,)),
                dma((nz,)),
                dma((STEPS, 2)),
                dma((STEPS, 2)),
                dma((STEPS, 2, hops, PARTS)),
                dma((STEPS, 2, hops, PARTS)),
                dma((STEPS, PARTS)),
                dma((STEPS, PARTS)),
            ],
            compiler_params=pltpu.CompilerParams(
                collective_id=0, has_side_effects=True, vmem_limit_bytes=60 * 1024 * 1024
            ),
        )(
            sigma_table,
            timesteps,
            frame_index,
            pfreq,
            tfreq,
            states,
            jnp.transpose(w_qkv, (1, 0, 2)),
            jnp.transpose(w_mod, (1, 0, 2)),
            w_out,
            noise,
        )

    in_specs = (
        P("queue", "head"),
        P(None, "head"),
        P("queue", None, "head"),
        P("head", None),
        P(None, None, "head"),
        P(),
        P(),
        P(),
    )
    out_specs = (P("queue", "head"), P("queue", "head"))
    return jax.shard_map(shards, mesh=mesh, in_specs=in_specs, out_specs=out_specs, check_vma=False)
```
